256 devices in a mesh: gx: 16 (over y, z_hi), gy: 4 (over x), gz: 4 (over z_lo, core).
Axes of the slice: x: 4, y: 4, z: 8 (z_hi: 4, z_lo: 2; z = z_hi * 2 + z_lo), core: 2. Of those that a mesh axis runs over, the one named last changes fastest.
Arguments:
- slab: float32 [672, 672, 512], P('gx', 'gy', 'gz'), may hold values from -36 to 36
- start_one: float32 [672, 96], replicated, may hold values from -6 to 6
- start_two: float32 [672, 96], replicated, may hold values from -6 to 6
Outputs:
- factor_one: float32 [672, 96], replicated
- factor_two: float32 [672, 96], replicated
- core: float32 [96, 96, 512], P('gx', 'gy', 'gz')
The draws below stay inside these ranges and needn't reach their ends.
All inputs are finite; a program needn't handle non-finite values.
Results may differ from the reference program's by a relative error of at most 0.0003.
Values sent between devices are 32-bit elements; how exact they have to be, the bound alone decides.
A program may use at most 128 MiB of HBM per device.

```python
import math
import jax
import jax.numpy as jnp
from jax import lax

N1 = 672
N2 = 672
RANK = 96
ITERS = 8
COLS = 512


def draw_slab(key, part):
    key = jax.random.fold_in(key, 11)
    first_key, second_key, value_key = jax.random.split(key, 3)
    top = math.log(3.0)
    values = jax.random.truncated_normal(value_key, -4.0, 4.0, (N1, N2, COLS), jnp.float32)
    row_scale = jnp.exp(jax.random.uniform(first_key, (N1, 1, 1), jnp.float32, 0.0, top))
    column_scale = jnp.exp(jax.random.uniform(second_key, (1, N2, 1), jnp.float32, 0.0, top))
    return (values * row_scale * column_scale).astype(jnp.float32)


def normal_values(own_key, dims, deviation, most, held_as=jnp.bfloat16):
    drawn = deviation * jax.random.normal(own_key, dims, jnp.float32)
    return jnp.clip(drawn, min=-most, max=most).astype(held_as)


def setup_inputs(seed: int = 0) -> dict:
    splits = jax.random.split(jax.random.key(seed), 4)
    return {
        "slab": draw_slab(jax.random.fold_in(splits[3], 71), 0),
        "start_one": normal_values(splits[1], (N1, RANK), 1.0, 6.0, jnp.float32),
        "start_two": normal_values(splits[2], (N2, RANK), 1.0, 6.0, jnp.float32),
    }


precise = lax.Precision.HIGHEST

def orthonormal(matrix):
    square = jnp.dot(matrix.T, matrix, precision=precise)
    factor = jnp.linalg.cholesky(square)
    return lax.linalg.triangular_solve(factor, matrix, left_side=False, lower=True, transpose_a=True)

def subspace(gram, basis):
    for sweep_index in range(ITERS):
        basis = orthonormal(jnp.dot(gram, basis, precision=precise))
    return basis

def reference(slab, start_one, start_two):
    flat = slab.reshape(N1, N2 * COLS)
    gram_one = jnp.dot(flat, flat.T, precision=precise) / (N2 * COLS)
    factor_one = subspace(gram_one, start_one)
    partial_core = jnp.einsum('ir,ijc->rjc', factor_one, slab, precision=precise)
    gram_two = jnp.einsum('rjc,rkc->jk', partial_core, partial_core, precision=precise) / (RANK * COLS)
    factor_two = subspace(gram_two, start_two)
    core = jnp.einsum('rjc,js->rsc', partial_core, factor_two, precision=precise)
    return (factor_one, factor_two, core)
```

```python
import functools
import jax
import jax.numpy as jnp
from jax import lax
from jax.experimental import pallas as pl
from jax.experimental.pallas import tpu as pltpu
from jax.sharding import PartitionSpec as P


RANK = 96
BAND = 96
BANDS = 7
ITERS = 8


def split(value):
    high = value.astype(jnp.bfloat16)
    low = (value - high.astype(jnp.float32)).astype(jnp.bfloat16)
    return high, low


def nt(a, b):
    return lax.dot_general(a, b, (((1,), (1,)), ((), ())), preferred_element_type=jnp.float32)


def tn(a, b):
    return lax.dot_general(a, b, (((0,), (0,)), ((), ())), preferred_element_type=jnp.float32)


def nn(a, b):
    return lax.dot_general(a, b, (((1,), (0,)), ((), ())), preferred_element_type=jnp.float32)


def spread_lanes(column):
    return jnp.broadcast_to(column, (8, 128))


def inverse_factor(square):
    rows = [square[8 * t : 8 * t + 8, :] for t in range(12)]
    lane = lax.broadcasted_iota(jnp.int32, (8, 128), 1)
    sub = lax.broadcasted_iota(jnp.int32, (8, 128), 0)
    aside = [(lane == sub + 8 * t).astype(jnp.float32) for t in range(12)]
    done = []
    for t in range(12):
        first = 8 * t
        tile, extra = rows[t], aside[t]
        cell = {
            (j, l): jnp.broadcast_to(tile[j : j + 1, first + l : first + l + 1], (8, 128))
            for j in range(8)
            for l in range(j + 1)
        }
        line = [jnp.broadcast_to(tile[j : j + 1, :], (8, 128)) for j in range(8)]
        side = [jnp.broadcast_to(extra[j : j + 1, :], (8, 128)) for j in range(8)]
        inv = []
        for l in range(8):
            flip = 1.0 / cell[l, l]
            inv.append(flip)
            for j in range(l + 1, 8):
                times = cell[j, l] * flip
                for m in range(l + 1, j + 1):
                    cell[j, m] = cell[j, m] - times * cell[m, l]
                line[j] = line[j] - times * line[l]
                side[j] = side[j] - times * side[l]
        out = side[0] * lax.rsqrt(cell[0, 0])
        for j in range(1, 8):
            out = jnp.where(sub == j, side[j] * lax.rsqrt(cell[j, j]), out)
        done.append(out)
        for u in range(t + 1, 12):
            tail, more = rows[u], aside[u]
            old = tail
            cols = []
            for l in range(8):
                value = spread_lanes(old[:, first + l : first + l + 1])
                for p in range(l):
                    value = value - cols[p] * cell[l, p]
                cols.append(value * inv[l])
            for l in range(8):
                tail = tail - cols[l] * line[l]
                more = more - cols[l] * side[l]
            rows[u], aside[u] = tail, more
    return jnp.concatenate(done, axis=0)


def subspace_kernel(scale, tiles_ref, start_ref, out_ref, ghi, glo, zcat):
    ghi[...] = jnp.zeros_like(ghi)
    glo[...] = jnp.zeros_like(glo)
    zcat[...] = jnp.zeros_like(zcat)
    for b in range(BANDS):
        parts = [
            tiles_ref[b * 36 + l * 12 : b * 36 + l * 12 + 12].reshape(BAND, 128) for l in range(3)
        ]
        strip = jnp.concatenate(parts, axis=1) * scale
        for m in range(4):
            block = strip[:, BAND * m : BAND * m + BAND]
            c = (b + m) % BANDS
            high, low = split(block)
            ghi[BAND * b : BAND * b + BAND, 128 * c : 128 * c + BAND] = high
            glo[BAND * b : BAND * b + BAND, 128 * c : 128 * c + BAND] = low
            if m:
                high, low = split(block.T)
                ghi[BAND * c : BAND * c + BAND, 128 * b : 128 * b + BAND] = high
                glo[BAND * c : BAND * c + BAND, 128 * b : 128 * b + BAND] = low

    def keep(value):
        high, low = split(value)
        for b in range(BANDS):
            zcat[128 * b : 128 * b + BAND, 0:128] = high[BAND * b : BAND * b + BAND]
            zcat[128 * b : 128 * b + BAND, 128:256] = low[BAND * b : BAND * b + BAND]

    def times_gram():
        both = nn(ghi[...], zcat[...])
        return both[:, 0:128] + both[:, 128:256] + nn(glo[...], zcat[:, 0:128])

    def factor():
        quad = tn(zcat[...], zcat[...])
        square = quad[0:128, 0:128] + quad[0:128, 128:256] + quad[128:256, 0:128] + quad[128:256, 128:256]
        return inverse_factor(square[0:RANK])

    def apply(value, inverse):
        high, low = split(value)
        mhi, mlo = split(jnp.concatenate([inverse, jnp.zeros((32, 128), jnp.float32)], axis=0))
        lhs = jnp.concatenate([high, low], axis=1)
        both = nt(lhs, jnp.concatenate([mhi, mhi], axis=1))
        return both + nt(high, mlo)

    start = jnp.concatenate([start_ref[...], jnp.zeros((672, 32), jnp.float32)], axis=1)
    keep(start)
    keep(times_gram())

    def step(_, carry):
        value = times_gram()
        keep(apply(value, factor()))
        return carry

    lax.fori_loop(0, ITERS - 1, step, 0)
    inverse = factor()
    high, low = [], []
    for b in range(BANDS):
        high.append(zcat[128 * b : 128 * b + BAND, 0:128])
        low.append(zcat[128 * b : 128 * b + BAND, 128:256])
    high = jnp.concatenate(high, axis=0)
    low = jnp.concatenate(low, axis=0)
    mhi, mlo = split(jnp.concatenate([inverse, jnp.zeros((32, 128), jnp.float32)], axis=0))
    lhs = jnp.concatenate([high, low], axis=1)
    out = nt(lhs, jnp.concatenate([mhi, mhi], axis=1)) + nt(high, mlo)
    out_ref[...] = out[:, 0:RANK]


def subspace(tiles, start, scale):
    return pl.pallas_call(
        functools.partial(subspace_kernel, scale),
        out_shape=jax.ShapeDtypeStruct((672, RANK), jnp.float32),
        in_specs=[pl.BlockSpec(memory_space=pltpu.VMEM)] * 2,
        out_specs=pl.BlockSpec(memory_space=pltpu.VMEM),
        scratch_shapes=[
            pltpu.VMEM((672, 896), jnp.bfloat16),
            pltpu.VMEM((672, 896), jnp.bfloat16),
            pltpu.VMEM((896, 256), jnp.bfloat16),
        ],
        compiler_params=pltpu.CompilerParams(vmem_limit_bytes=48 * 2**20),
        name="subspace",
    )(tiles, start)


MESH = pl.DeviceIdType.MESH


def place():
    gx, gy, gz = lax.axis_index("gx"), lax.axis_index("gy"), lax.axis_index("gz")
    x, y = gy, gx // 4
    z = (gx % 4) * 2 + gz // 2
    return x, y, z, gz % 2


def device(x, y, z, core):
    return (y * 4 + z // 2, x, (z % 2) * 2 + core)


def turn(value, by, size):
    return lax.rem(value + by, size)


def sum_everywhere(tiles, out, half, first, second, third, fourth, send, recv):
    x, y, z, core = place()
    flip = core == 0
    a = jnp.where(flip, x, y)
    b = jnp.where(flip, y, x)

    def at(pa, pb, pz, pc):
        return device(jnp.where(flip, pa, pb), jnp.where(flip, pb, pa), pz, pc)

    partner = at(a, b, z, 1 - core)
    peers_a = [at(turn(a, d, 4), b, z, core) for d in range(1, 4)]
    peers_b = [at(a, turn(b, d, 4), z, core) for d in range(1, 4)]
    peers_z = [at(a, b, turn(z, d, 8), core) for d in range(1, 8)]

    def copy(src, dst, sem, to):
        c = pltpu.make_async_remote_copy(
            src_ref=src, dst_ref=dst, send_sem=send.at[sem], recv_sem=recv.at[sem],
            device_id=to, device_id_type=MESH)
        c.start()
        return c

    mine = core * 128
    other = (1 - core) * 128
    c = copy(tiles.at[pl.ds(other, 128)], first, 0, partner)
    c.wait()
    half[...] = tiles[pl.ds(mine, 128)] + first[...]
    cs = [copy(half.at[pl.ds(turn(a, d, 4) * 32, 32)], second.at[d - 1], d, peers_a[d - 1]) for d in range(1, 4)]
    for c in cs:
        c.wait()
    mine_a = a * 32
    half[pl.ds(mine_a, 32)] = half[pl.ds(mine_a, 32)] + second[0] + second[1] + second[2]
    cs = [copy(half.at[pl.ds(mine_a + turn(b, d, 4) * 8, 8)], third.at[d - 1], 3 + d, peers_b[d - 1]) for d in range(1, 4)]
    for c in cs:
        c.wait()
    mine_b = mine_a + b * 8
    half[pl.ds(mine_b, 8)] = half[pl.ds(mine_b, 8)] + third[0] + third[1] + third[2]
    cs = [copy(half.at[mine_b + turn(z, d, 8)], fourth.at[d - 1], 6 + d, peers_z[d - 1]) for d in range(1, 8)]
    for c in cs:
        c.wait()
    own = mine_b + z
    total = half[own]
    for d in range(7):
        total = total + fourth[d]
    out[mine + own] = total
    cs = [copy(out.at[mine + own], out.at[mine + own], 13 + d, peers_z[d - 1]) for d in range(1, 8)]
    for c in cs:
        c.wait()
    block = out.at[pl.ds(mine + mine_b, 8)]
    cs = [copy(block, block, 20 + d, peers_b[d - 1]) for d in range(1, 4)]
    for c in cs:
        c.wait()
    block = out.at[pl.ds(mine + mine_a, 32)]
    cs = [copy(block, block, 23 + d, peers_a[d - 1]) for d in range(1, 4)]
    for c in cs:
        c.wait()
    block = out.at[pl.ds(mine, 128)]
    c = copy(block, block, 27, partner)
    c.wait()


def greet():
    x, y, z, core = place()
    barrier = pltpu.get_barrier_semaphore()
    ids = [device(x, y, z, 1 - core)]
    ids += [device(turn(x, d, 4), y, z, core) for d in range(1, 4)]
    ids += [device(x, turn(y, d, 4), z, core) for d in range(1, 4)]
    ids += [device(x, y, turn(z, d, 8), core) for d in range(1, 8)]
    for i in ids:
        pl.semaphore_signal(barrier, inc=1, device_id=i, device_id_type=MESH)
    pl.semaphore_wait(barrier, len(ids))


def partial_gram(x_ref, xhi, xlo, tiles):
    high, low = split(x_ref[...])
    xhi[0:672], xlo[0:672] = high, low
    xhi[672:960], xlo[672:960] = high[0:288], low[0:288]
    tiles[252:256] = jnp.zeros((4, 8, 128), jnp.float32)
    for b in range(BANDS):
        i = pl.ds(BAND * b, BAND)
        k = pl.ds(BAND * b, 4 * BAND)
        strip = nt(xhi[i], xhi[k]) + nt(xhi[i], xlo[k]) + nt(xlo[i], xhi[k])
        for l in range(3):
            t = b * 36 + l * 12
            tiles[t : t + 12] = strip[:, 128 * l : 128 * l + 128].reshape(12, 8, 128)


def gram_kernel(x_ref, out, xhi, xlo, tiles, half, first, second, third, fourth, send, recv):
    greet()
    partial_gram(x_ref, xhi, xlo, tiles)
    sum_everywhere(tiles, out, half, first, second, third, fourth, send, recv)


def gram(x, collective_id):
    f32 = jnp.float32
    k = x.shape[1]
    return pl.pallas_call(
        gram_kernel,
        out_shape=jax.ShapeDtypeStruct((256, 8, 128), f32),
        in_specs=[pl.BlockSpec(memory_space=pltpu.VMEM)],
        out_specs=pl.BlockSpec(memory_space=pltpu.VMEM),
        scratch_shapes=[
            pltpu.VMEM((960, k), jnp.bfloat16),
            pltpu.VMEM((960, k), jnp.bfloat16),
            pltpu.VMEM((256, 8, 128), f32),
            pltpu.VMEM((128, 8, 128), f32),
            pltpu.VMEM((128, 8, 128), f32),
            pltpu.VMEM((3, 32, 8, 128), f32),
            pltpu.VMEM((3, 8, 8, 128), f32),
            pltpu.VMEM((7, 8, 128), f32),
            pltpu.SemaphoreType.DMA((28,)),
            pltpu.SemaphoreType.DMA((28,)),
        ],
        compiler_params=pltpu.CompilerParams(
            collective_id=collective_id, has_side_effects=True, vmem_limit_bytes=48 * 2**20),
        name="gram_sum",
    )(x)


precise = lax.Precision.HIGHEST


def body(slab, start_one, start_two):
    gy_count = lax.axis_size("gy")
    gz_count = lax.axis_size("gz")
    row_count, col_block, depth = slab.shape
    rank_total = start_one.shape[1]
    spread = lax.all_to_all(
        slab.reshape(row_count, col_block * depth), "gx", split_axis=1, concat_axis=0, tiled=True
    )
    scale_one = 1.0 / (col_block * gy_count * depth * gz_count)
    factor_one = subspace(gram(spread, 0), start_one, scale_one)
    local = lax.dot_general(
        factor_one, spread, (((0,), (0,)), ((), ())), precision=precise
    )
    partial_core = lax.all_to_all(local, "gx", split_axis=0, concat_axis=1, tiled=True)
    partial_core = partial_core.reshape(-1, col_block, depth)
    spread_second = lax.all_to_all(partial_core, "gy", split_axis=2, concat_axis=1, tiled=True)
    flat = spread_second.transpose(1, 0, 2).reshape(col_block * gy_count, -1)
    scale_two = 1.0 / (rank_total * depth * gz_count)
    factor_two = subspace(gram(flat, 1), start_two, scale_two)
    own_second = lax.dynamic_slice_in_dim(
        factor_two, lax.axis_index("gy") * col_block, col_block, 0
    )
    core_terms = jnp.einsum("rjc,js->rsc", partial_core, own_second, precision=precise)
    core = lax.psum_scatter(core_terms, "gy", scatter_dimension=1, tiled=True)
    return (factor_one, factor_two, core)


def solution(mesh):
    placed = (P("gx", "gy", "gz"), P(), P())
    return jax.shard_map(
        body, mesh=mesh, in_specs=placed, out_specs=(P(), P(), P("gx", "gy", "gz")), check_vma=False
    )
```

```python
import functools
import jax
import jax.numpy as jnp
from jax import lax
from jax.experimental import pallas as pl
from jax.experimental.pallas import tpu as pltpu
from jax.sharding import PartitionSpec as P

RANK = 96
ROWS = 672
ITERS = 8
OWN = 42
LANES = 128
MESH = pl.DeviceIdType.MESH
F32 = jnp.float32
BF16 = jnp.bfloat16
COUNT = (84, 68, 52, 36, 16)
BASE = (0, 84, 152, 204, 240)


def split(value):
    high = value.astype(BF16)
    low = (value - high.astype(F32)).astype(BF16)
    return high, low


def dot(a, b, left, right):
    return lax.dot_general(a, b, (((left,), (right,)), ((), ())), preferred_element_type=F32)


def nt(a, b):
    return dot(a, b, 1, 1)


def nn(a, b):
    return dot(a, b, 1, 0)


def vmem(count):
    return [pl.BlockSpec(memory_space=pltpu.VMEM)] * count


def inverse_factor(square):
    rows = [square[8 * t : 8 * t + 8, :] for t in range(12)]
    lane = lax.broadcasted_iota(jnp.int32, (8, 128), 1)
    sub = lax.broadcasted_iota(jnp.int32, (8, 128), 0)
    aside = [(lane == sub + 8 * t).astype(F32) for t in range(12)]
    done = []
    for t in range(12):
        first = 8 * t
        tile, extra = rows[t], aside[t]
        cell = {
            (j, l): jnp.broadcast_to(tile[j : j + 1, first + l : first + l + 1], (8, 128))
            for j in range(8)
            for l in range(j + 1)
        }
        line = [jnp.broadcast_to(tile[j : j + 1, :], (8, 128)) for j in range(8)]
        side = [jnp.broadcast_to(extra[j : j + 1, :], (8, 128)) for j in range(8)]
        inv = []
        for l in range(8):
            flip = 1.0 / cell[l, l]
            inv.append(flip)
            for j in range(l + 1, 8):
                times = cell[j, l] * flip
                for m in range(l + 1, j + 1):
                    cell[j, m] = cell[j, m] - times * cell[m, l]
                line[j] = line[j] - times * line[l]
                side[j] = side[j] - times * side[l]
        out = side[0] * lax.rsqrt(cell[0, 0])
        for j in range(1, 8):
            out = jnp.where(sub == j, side[j] * lax.rsqrt(cell[j, j]), out)
        done.append(out)
        for u in range(t + 1, 12):
            tail, more = rows[u], aside[u]
            old = tail
            cols = []
            for l in range(8):
                value = jnp.broadcast_to(old[:, first + l : first + l + 1], (8, 128))
                for p in range(l):
                    value = value - cols[p] * cell[l, p]
                cols.append(value * inv[l])
            for l in range(8):
                tail = tail - cols[l] * line[l]
                more = more - cols[l] * side[l]
            rows[u], aside[u] = tail, more
    return jnp.concatenate(done, axis=0)


def subspace_kernel(scale, tiles_ref, start_ref, out_ref, ghi, glo, zcat):
    def put(r, c, value):
        high, low = split(value)
        ghi[r : r + value.shape[0], c : c + value.shape[1]] = high
        glo[r : r + value.shape[0], c : c + value.shape[1]] = low

    row = lax.broadcasted_iota(jnp.int32, (128, 128), 0)
    col = lax.broadcasted_iota(jnp.int32, (128, 128), 1)
    corner = []
    for l in range(5):
        n = COUNT[l] * 8
        block = tiles_ref[BASE[l] : BASE[l] + COUNT[l]].reshape(n, 128) * scale
        diag = block[0:128]
        put(128 * l, 128 * l, jnp.where(row >= col, diag, diag.T))
        corner.append(pltpu.roll(diag[0:32], (32 + 32 * l) % 128, 1))
        if l < 4:
            rest = block[128:]
            put(128 * l + 128, 128 * l, rest)
            tall = jnp.concatenate([rest, jnp.zeros((96, 128), F32)], axis=0)
            put(128 * l, 128 * l + 128, tall.T)
    lane = lax.broadcasted_iota(jnp.int32, (32, 128), 1)
    left = corner[0]
    for l in range(1, 4):
        left = jnp.where(lane >= 32 * l, corner[l], left)
    right = jnp.where(lane < 32, corner[4], 0.0)
    put(640, 512, left)
    put(640, 640, right)
    put(512, 640, jnp.concatenate([left, jnp.zeros((96, 128), F32)], axis=0).T)
    zcat[ROWS:768] = jnp.zeros((96, 256), BF16)

    def keep(value):
        high, low = split(value)
        zcat[0:ROWS, 0:128] = high
        zcat[0:ROWS, 128:256] = low

    def times_gram():
        both = nn(ghi[...], zcat[...])
        return both[:, 0:128] + both[:, 128:256] + nn(glo[...], zcat[:, 0:128])

    def factor():
        z = zcat[0:ROWS]
        quad = dot(z, z, 0, 0)
        square = quad[0:128, 0:128] + quad[0:128, 128:256] + quad[128:256, 0:128] + quad[128:256, 128:256]
        return inverse_factor(square[0:RANK])

    def apply(high, low, inverse):
        mhi, mlo = split(jnp.concatenate([inverse, jnp.zeros((32, 128), F32)], axis=0))
        lhs = jnp.concatenate([high, low], axis=1)
        return nt(lhs, jnp.concatenate([mhi, mhi], axis=1)) + nt(high, mlo)

    keep(jnp.concatenate([start_ref[...], jnp.zeros((ROWS, 32), F32)], axis=1))
    keep(times_gram())

    def step(_, carry):
        high, low = split(times_gram())
        keep(apply(high, low, factor()))
        return carry

    lax.fori_loop(0, ITERS - 1, step, 0)
    out = apply(zcat[0:ROWS, 0:128], zcat[0:ROWS, 128:256], factor())
    out_ref[...] = out[:, 0:RANK]


def subspace(tiles, start, scale):
    return pl.pallas_call(
        functools.partial(subspace_kernel, scale),
        out_shape=jax.ShapeDtypeStruct((ROWS, RANK), F32),
        in_specs=vmem(2),
        out_specs=vmem(1)[0],
        scratch_shapes=[
            pltpu.VMEM((ROWS, 768), BF16),
            pltpu.VMEM((ROWS, 768), BF16),
            pltpu.VMEM((768, 256), BF16),
        ],
        compiler_params=pltpu.CompilerParams(vmem_limit_bytes=48 * 2**20),
        name="subspace",
    )(tiles, start)


def place():
    gx, gy, gz = lax.axis_index("gx"), lax.axis_index("gy"), lax.axis_index("gz")
    return gy, gx // 4, (gx % 4) * 2 + gz // 2, gz % 2


def device(x, y, z, core):
    return (y * 4 + z // 2, x, (z % 2) * 2 + core)


def turn(value, by, size):
    return lax.rem(value + by, size)


def greet(ids):
    barrier = pltpu.get_barrier_semaphore()
    for i in ids:
        pl.semaphore_signal(barrier, inc=1, device_id=i, device_id_type=MESH)
    return len(ids)


def remote(src, dst, send, recv, to):
    copy = pltpu.make_async_remote_copy(
        src_ref=src, dst_ref=dst, send_sem=send, recv_sem=recv, device_id=to, device_id_type=MESH
    )
    copy.start()
    return copy


def local(src, dst, sem):
    pltpu.make_async_copy(src, dst, sem).start()


def await_all(ref, sem):
    pltpu.make_async_copy(ref, ref, sem).wait()


SUM_SCRATCH = [
    pltpu.VMEM((256, 8, 128), F32),
    pltpu.VMEM((128, 8, 128), F32),
    pltpu.VMEM((128, 8, 128), F32),
    pltpu.VMEM((3, 32, 8, 128), F32),
    pltpu.VMEM((3, 8, 8, 128), F32),
    pltpu.VMEM((7, 8, 128), F32),
    pltpu.SemaphoreType.DMA((28,)),
    pltpu.SemaphoreType.DMA((28,)),
]


def sum_everywhere(out, tiles, half, first, second, third, fourth, send, recv):
    x, y, z, core = place()
    flip = core == 0
    a = jnp.where(flip, x, y)
    b = jnp.where(flip, y, x)

    def at(pa, pb, pz, pc):
        return device(jnp.where(flip, pa, pb), jnp.where(flip, pb, pa), pz, pc)

    partner = at(a, b, z, 1 - core)
    peers_a = [at(turn(a, d, 4), b, z, core) for d in range(1, 4)]
    peers_b = [at(a, turn(b, d, 4), z, core) for d in range(1, 4)]
    peers_z = [at(a, b, turn(z, d, 8), core) for d in range(1, 8)]

    def copy(src, dst, sem, to):
        return remote(src, dst, send.at[sem], recv.at[sem], to)

    def wait(copies):
        for c in copies:
            c.wait()

    mine = core * 128
    other = (1 - core) * 128
    wait([copy(tiles.at[pl.ds(other, 128)], first, 0, partner)])
    half[...] = tiles[pl.ds(mine, 128)] + first[...]
    wait([copy(half.at[pl.ds(turn(a, d, 4) * 32, 32)], second.at[d - 1], d, peers_a[d - 1]) for d in range(1, 4)])
    mine_a = a * 32
    half[pl.ds(mine_a, 32)] = half[pl.ds(mine_a, 32)] + second[0] + second[1] + second[2]
    wait([
        copy(half.at[pl.ds(mine_a + turn(b, d, 4) * 8, 8)], third.at[d - 1], 3 + d, peers_b[d - 1])
        for d in range(1, 4)
    ])
    mine_b = mine_a + b * 8
    half[pl.ds(mine_b, 8)] = half[pl.ds(mine_b, 8)] + third[0] + third[1] + third[2]
    wait([copy(half.at[mine_b + turn(z, d, 8)], fourth.at[d - 1], 6 + d, peers_z[d - 1]) for d in range(1, 8)])
    own = mine_b + z
    total = half[own]
    for d in range(7):
        total = total + fourth[d]
    out[mine + own] = total
    wait([copy(out.at[mine + own], out.at[mine + own], 13 + d, peers_z[d - 1]) for d in range(1, 8)])
    block = out.at[pl.ds(mine + mine_b, 8)]
    wait([copy(block, block, 20 + d, peers_b[d - 1]) for d in range(1, 4)])
    block = out.at[pl.ds(mine + mine_a, 32)]
    wait([copy(block, block, 23 + d, peers_a[d - 1]) for d in range(1, 4)])
    block = out.at[pl.ds(mine, 128)]
    wait([copy(block, block, 27, partner)])


def add_gram(hi, lo, tiles, fresh):
    def put(l, skip, value):
        n = value.shape[0] // 8
        at = pl.ds(BASE[l] + skip // 8, n)
        value = value.reshape(n, 8, 128)
        tiles[at] = value if fresh else tiles[at] + value

    def product(r, c, n):
        return nt(hi[r:], hi[c : c + n]) + nt(hi[r:], lo[c : c + n]) + nt(lo[r:], hi[c : c + n])

    last = product(512, 512, 160)
    lane = lax.broadcasted_iota(jnp.int32, (32, 128), 1)

    def corner(l, value):
        tail = last[128:160, 0:128]
        if l == 4:
            tail = jnp.concatenate([last[128:160, 128:160], jnp.zeros((32, 96), F32)], axis=1)
        tail = pltpu.roll(tail, (96 - 32 * (l % 4)) % 128, 1)
        put(l, 0, jnp.where(lane >= 96, tail, value[0:32]))
        put(l, 32, value[32:])

    block = product(0, 0, 256)
    corner(0, block[:, 0:128])
    corner(1, block[128:, 128:256])
    block = product(256, 256, 256)
    corner(2, block[:, 0:128])
    corner(3, block[128:, 128:256])
    corner(4, last[0:128, 0:128])


def extra_tile():
    gx, gz = lax.axis_index("gx"), lax.axis_index("gz")
    y, z = gx // 4, gx % 4
    n = 4 * z + y
    usual = n // 5 == gz
    has = jnp.logical_or(usual, jnp.logical_and(z == 0, gz == 3))
    return has, jnp.where(usual, n - 5 * gz, 1 + y)


def first_kernel(slab, out, xhi, xlo, rows, tiles, half, first, second, third, fourth, send, recv,
                 slab_send, more_send, slab_recv):
    gx, gy, gz = lax.axis_index("gx"), lax.axis_index("gy"), lax.axis_index("gz")
    x, y, z, core = place()
    ids = [(turn(gx, d, 16), gy, gz) for d in range(1, 16)]
    ids += [device(x, y, z, 1 - core)]
    ids += [device(turn(x, d, 4), y, z, core) for d in range(1, 4)]
    ids += [device(x, y, turn(z, d, 8), core) for d in (1, 3, 5, 7)]
    pl.semaphore_wait(pltpu.get_barrier_semaphore(), greet(ids))

    mine = pl.ds(gx * OWN, OWN)
    copies = []
    for d in range(1, 16):
        to = turn(gx, d, 16)
        copies.append(remote(slab.at[:, pl.ds(to * 8, 8)], rows.at[0, mine], slab_send.at[d],
                             slab_recv.at[0], (to, gy, gz)))
    local(slab.at[:, pl.ds(gx * 8, 8)], rows.at[0, mine], slab_recv.at[0])
    for e in range(5):
        n = 5 * gz + e
        to = (n % 4) * 4 + (n // 4) % 4
        src = slab.at[:, pl.ds(128 + 8 * e, 8)]

        @pl.when(to != gx)
        def _():
            remote(src, rows.at[1, mine], more_send.at[e], slab_recv.at[1], (to, gy, gz))

        @pl.when(to == gx)
        def _():
            local(src, rows.at[1, mine], slab_recv.at[1])

    def use(p):
        for j in range(8):
            high, low = split(rows[p, :, j, :])
            xhi[p, :, 128 * j : 128 * j + 128] = high
            xlo[p, :, 128 * j : 128 * j + 128] = low
        add_gram(xhi.at[p], xlo.at[p], tiles, p == 0)

    await_all(rows.at[0], slab_recv.at[0])
    use(0)
    has, _ = extra_tile()

    @pl.when(has)
    def _():
        await_all(rows.at[1], slab_recv.at[1])
        use(1)

    for c in copies:
        c.wait_send()
    for e in range(5):
        n = 5 * gz + e
        to = (n % 4) * 4 + (n // 4) % 4

        @pl.when(to != gx)
        def _():
            src = slab.at[:, pl.ds(128 + 8 * e, 8)]
            await_all(src, more_send.at[e])

    sum_everywhere(out, tiles, half, first, second, third, fourth, send, recv)


def first_gram(slab):
    return pl.pallas_call(
        first_kernel,
        out_shape=(
            jax.ShapeDtypeStruct((256, 8, 128), F32),
            jax.ShapeDtypeStruct((2, ROWS, 1024), BF16),
            jax.ShapeDtypeStruct((2, ROWS, 1024), BF16),
        ),
        in_specs=[pl.BlockSpec(memory_space=pltpu.MemorySpace.HBM)],
        out_specs=tuple(vmem(3)),
        scratch_shapes=[
            pltpu.VMEM((2, ROWS, 8, 128), F32),
            *SUM_SCRATCH,
            pltpu.SemaphoreType.DMA((16,)),
            pltpu.SemaphoreType.DMA((5,)),
            pltpu.SemaphoreType.DMA((2,)),
        ],
        compiler_params=pltpu.CompilerParams(
            collective_id=0, has_side_effects=True, vmem_limit_bytes=48 * 2**20),
        name="first_gram",
    )(slab)


def ranks(gy, core):
    low = gy < 2
    if_zero = (jnp.where(low, 2 * gy, gy + 2), jnp.where(low, 2, 1))
    if_one = (jnp.where(low, gy, 2 * gy - 2), jnp.where(low, 1, 2))
    return jnp.where(core == 0, if_zero[0], if_one[0]), jnp.where(core == 0, if_zero[1], if_one[1])


def owner(r, core):
    zero = (jnp.where(r < 4, r // 2, r - 2), jnp.where(r < 4, r % 2, 0))
    one = (jnp.where(r < 2, r, r // 2 + 1), jnp.where(r < 2, 0, r % 2))
    return jnp.where(core == 0, zero[0], one[0]), jnp.where(core == 0, zero[1], one[1])


def basis_rows(basis):
    wide = jnp.concatenate([basis, jnp.zeros((ROWS, 32), F32)], axis=1)
    high, low = split(wide.T[0:RANK])
    return jnp.concatenate([high, low], axis=0)


def contract(stacked, hi, lo):
    both = nn(stacked, hi)
    return both[0:RANK] + both[RANK:] + nn(stacked[0:RANK], lo)


def second_kernel(basis, xhi, xlo, out, qhi, qlo, part, rows, tiles, half, first, second, third, fourth,
                  send, recv, part_send, part_recv):
    gx, gy, gz = lax.axis_index("gx"), lax.axis_index("gy"), lax.axis_index("gz")
    x, y, z, core = place()
    barrier = pltpu.get_barrier_semaphore()

    def hello(i, carry):
        to = (turn(gx, i // 4, 16), turn(gy, i % 4, 4), gz)
        pl.semaphore_signal(barrier, inc=1, device_id=to, device_id_type=MESH)
        return carry

    lax.fori_loop(1, 64, hello, 0)
    ids = [device(x, y, z, 1 - core)] + [device(x, y, turn(z, d, 8), core) for d in (1, 3, 5, 7)]
    count = 63 + greet(ids)
    stacked = basis_rows(basis[...])
    has, which = extra_tile()

    def work(p):
        for j in range(0, 8, 2):
            at = pl.ds(128 * j, 256)
            value = contract(stacked, xhi[p, :, at], xlo[p, :, at])
            part[p, :, j, :] = value[:, 0:128]
            part[p, :, j + 1, :] = value[:, 128:256]

    def deal(p, tile):
        at = pl.ds(gy * 168 + tile * 8, 8)

        def one(r, carry):
            to_x = r // 6
            to_y, slot = owner(r % 6, core)
            me = jnp.logical_and(to_x == gx, to_y == gy)

            @pl.when(jnp.logical_not(me))
            def _():
                remote(part.at[p, r], rows.at[slot, at], part_send.at[p], part_recv.at[0], (to_x, to_y, gz))

            @pl.when(me)
            def _():
                local(part.at[p, r], rows.at[slot, at], part_recv.at[0])

            return carry

        lax.fori_loop(0, RANK, one, 0)

    work(0)
    pl.semaphore_wait(barrier, count)
    deal(0, gx)

    @pl.when(has)
    def _():
        work(1)
        deal(1, 16 + which)

    _, held = ranks(gy, core)

    @pl.when(held == 2)
    def _():
        await_all(rows, part_recv.at[0])
        await_all(part.at[0, pl.ds(0, 94)], part_send.at[0])

        @pl.when(has)
        def _():
            await_all(part.at[1, pl.ds(0, 94)], part_send.at[1])

        high, low = split(rows[1])
        qhi[:, 128:256] = high
        qlo[:, 128:256] = low

    @pl.when(held != 2)
    def _():
        await_all(rows.at[0], part_recv.at[0])
        await_all(part.at[0, pl.ds(0, 95)], part_send.at[0])

        @pl.when(has)
        def _():
            await_all(part.at[1, pl.ds(0, 95)], part_send.at[1])

        qhi[:, 128:256] = jnp.zeros((ROWS, 128), BF16)
        qlo[:, 128:256] = jnp.zeros((ROWS, 128), BF16)

    high, low = split(rows[0])
    qhi[:, 0:128] = high
    qlo[:, 0:128] = low
    add_gram(qhi, qlo, tiles, True)
    sum_everywhere(out, tiles, half, first, second, third, fourth, send, recv)


def second_gram(basis, xhi, xlo):
    return pl.pallas_call(
        second_kernel,
        out_shape=(
            jax.ShapeDtypeStruct((256, 8, 128), F32),
            jax.ShapeDtypeStruct((ROWS, 256), BF16),
            jax.ShapeDtypeStruct((ROWS, 256), BF16),
        ),
        in_specs=vmem(3),
        out_specs=tuple(vmem(3)),
        scratch_shapes=[
            pltpu.VMEM((2, RANK, 8, 128), F32),
            pltpu.VMEM((2, ROWS, 128), F32),
            *SUM_SCRATCH,
            pltpu.SemaphoreType.DMA((2,)),
            pltpu.SemaphoreType.DMA((1,)),
        ],
        compiler_params=pltpu.CompilerParams(
            collective_id=1, has_side_effects=True, vmem_limit_bytes=48 * 2**20),
        name="second_gram",
    )(basis, xhi, xlo)


def core_kernel(basis, qhi, qlo, out, terms, send, recv):
    gx, gy, gz = lax.axis_index("gx"), lax.axis_index("gy"), lax.axis_index("gz")
    barrier = pltpu.get_barrier_semaphore()
    count = greet([(gx, turn(gy, d, 4), gz) for d in range(1, 4)])
    value = contract(basis_rows(basis[...]), qhi[...], qlo[...])
    terms[0] = value[:, 0:128]
    terms[1] = value[:, 128:256]
    start, held = ranks(gy, gz % 2)
    pl.semaphore_wait(barrier, count)

    def deal(k):
        dst = out.at[start + k]
        for d in range(1, 4):
            to = turn(gy, d, 4)
            remote(terms.at[k, pl.ds(to * 24, 24)], dst, send.at[k, d], recv.at[0], (gx, to, gz))
        local(terms.at[k, pl.ds(gy * 24, 24)], dst, recv.at[0])

    def finish(k):
        for d in range(1, 4):
            await_all(terms.at[k, pl.ds(0, 24)], send.at[k, d])

    deal(0)

    @pl.when(held == 2)
    def _():
        deal(1)
        finish(1)

    finish(0)
    await_all(out, recv.at[0])


def core_piece(basis, qhi, qlo):
    return pl.pallas_call(
        core_kernel,
        out_shape=jax.ShapeDtypeStruct((6, 24, 128), F32),
        in_specs=vmem(3),
        out_specs=vmem(1)[0],
        scratch_shapes=[
            pltpu.VMEM((2, RANK, 128), F32),
            pltpu.SemaphoreType.DMA((2, 4)),
            pltpu.SemaphoreType.DMA((1,)),
        ],
        compiler_params=pltpu.CompilerParams(
            collective_id=2, has_side_effects=True, vmem_limit_bytes=48 * 2**20),
        name="core_piece",
    )(basis, qhi, qlo)


def body(slab, start_one, start_two):
    tiles, xhi, xlo = first_gram(slab)
    factor_one = subspace(tiles, start_one, 1.0 / (672 * 512))
    tiles, qhi, qlo = second_gram(factor_one, xhi, xlo)
    factor_two = subspace(tiles, start_two, 1.0 / (RANK * 512))
    return factor_one, factor_two, core_piece(factor_two, qhi, qlo)


def solution(mesh):
    placed = (P("gx", "gy", "gz"), P(), P())
    return jax.shard_map(
        body, mesh=mesh, in_specs=placed, out_specs=(P(), P(), P("gx", "gy", "gz")), check_vma=False
    )
```

```python
import functools
import jax
import jax.numpy as jnp
from jax import lax
from jax.experimental import pallas as pl
from jax.experimental.pallas import tpu as pltpu
from jax.sharding import PartitionSpec as P

RANK = 96
ROWS = 672
ITERS = 8
OWN = 42
LANES = 128
MESH = pl.DeviceIdType.MESH
F32 = jnp.float32
BF16 = jnp.bfloat16
COUNT = (84, 68, 52, 36, 16)
BASE = (0, 84, 152, 204, 240)


def split(value):
    high = value.astype(BF16)
    low = (value - high.astype(F32)).astype(BF16)
    return high, low


def dot(a, b, left, right):
    return lax.dot_general(a, b, (((left,), (right,)), ((), ())), preferred_element_type=F32)


def nt(a, b):
    return dot(a, b, 1, 1)


def nn(a, b):
    return dot(a, b, 1, 0)


def vmem(count):
    return [pl.BlockSpec(memory_space=pltpu.VMEM)] * count


def inverse_factor(square):
    rows = [square[8 * t : 8 * t + 8, :] for t in range(12)]
    lane = lax.broadcasted_iota(jnp.int32, (8, 128), 1)
    sub = lax.broadcasted_iota(jnp.int32, (8, 128), 0)
    aside = [(lane == sub + 8 * t).astype(F32) for t in range(12)]
    done = []
    ahead = [jnp.broadcast_to(rows[0][:, l : l + 1], (8, 128)) for l in range(8)]
    for t in range(12):
        first = 8 * t
        tile, extra = rows[t], aside[t]
        wide = ahead
        cell, line, side, inv = {}, [], [], []
        pivots = None
        for l in range(8):
            for m in range(l, 8):
                cell[m, l] = jnp.broadcast_to(wide[m][l : l + 1, :], (8, 128))
            line.append(jnp.broadcast_to(tile[l : l + 1, :], (8, 128)))
            side.append(jnp.broadcast_to(extra[l : l + 1, :], (8, 128)))
            inv.append(1.0 / cell[l, l])
            pivots = cell[l, l] if l == 0 else jnp.where(sub == l, cell[l, l], pivots)
            if l < 7:
                times = jnp.where(sub > l, wide[l] * inv[l], 0.0)
                for m in range(l + 1, 8):
                    wide[m] = wide[m] - times * cell[m, l]
                tile = tile - times * line[l]
                extra = extra - times * side[l]
        out = extra * lax.rsqrt(pivots)
        done.append(out)
        for u in range(t + 1, 12):
            tail, more = rows[u], aside[u]
            raw, cols = [], []
            for l in range(8):
                value = jnp.broadcast_to(tail[:, first + l : first + l + 1], (8, 128))
                for p in range(l):
                    value = value - cols[p] * cell[l, p]
                raw.append(value)
                cols.append(value * inv[l])
            if u == t + 1:
                ahead = []
                for m in range(8):
                    value = jnp.broadcast_to(tail[:, first + 8 + m : first + 9 + m], (8, 128))
                    for l in range(8):
                        value = value - cols[l] * jnp.broadcast_to(raw[l][m : m + 1, :], (8, 128))
                    ahead.append(value)
            for l in range(8):
                tail = tail - cols[l] * line[l]
                more = more - cols[l] * side[l]
            rows[u], aside[u] = tail, more
    return jnp.concatenate(done, axis=0)


def subspace_kernel(scale, tiles_ref, start_ref, out_ref, ghi, glo, zcat):
    def put(r, c, value):
        high, low = split(value)
        ghi[r : r + value.shape[0], c : c + value.shape[1]] = high
        glo[r : r + value.shape[0], c : c + value.shape[1]] = low

    row = lax.broadcasted_iota(jnp.int32, (128, 128), 0)
    col = lax.broadcasted_iota(jnp.int32, (128, 128), 1)
    corner = []
    for l in range(5):
        n = COUNT[l] * 8
        block = tiles_ref[BASE[l] : BASE[l] + COUNT[l]].reshape(n, 128) * scale
        diag = block[0:128]
        put(128 * l, 128 * l, jnp.where(row >= col, diag, diag.T))
        corner.append(pltpu.roll(diag[0:32], (32 + 32 * l) % 128, 1))
        if l < 4:
            rest = block[128:]
            put(128 * l + 128, 128 * l, rest)
            tall = jnp.concatenate([rest, jnp.zeros((96, 128), F32)], axis=0)
            put(128 * l, 128 * l + 128, tall.T)
    lane = lax.broadcasted_iota(jnp.int32, (32, 128), 1)
    left = corner[0]
    for l in range(1, 4):
        left = jnp.where(lane >= 32 * l, corner[l], left)
    right = jnp.where(lane < 32, corner[4], 0.0)
    put(640, 512, left)
    put(640, 640, right)
    put(512, 640, jnp.concatenate([left, jnp.zeros((96, 128), F32)], axis=0).T)
    zcat[ROWS:768] = jnp.zeros((96, 256), BF16)

    def keep(value):
        high, low = split(value)
        zcat[0:ROWS, 0:128] = high
        zcat[0:ROWS, 128:256] = low

    def times_gram():
        both = nn(ghi[...], zcat[...])
        return both[:, 0:128] + both[:, 128:256] + nn(glo[...], zcat[:, 0:128])

    def factor():
        z = zcat[0:ROWS]
        quad = dot(z, z, 0, 0)
        square = quad[0:128, 0:128] + quad[0:128, 128:256] + quad[128:256, 0:128] + quad[128:256, 128:256]
        return inverse_factor(square[0:RANK])

    def apply(high, low, inverse):
        mhi, mlo = split(jnp.concatenate([inverse, jnp.zeros((32, 128), F32)], axis=0))
        lhs = jnp.concatenate([high, low], axis=1)
        return nt(lhs, jnp.concatenate([mhi, mhi], axis=1)) + nt(high, mlo)

    keep(jnp.concatenate([start_ref[...], jnp.zeros((ROWS, 32), F32)], axis=1))
    keep(times_gram())

    def step(_, carry):
        high, low = split(times_gram())
        keep(apply(high, low, factor()))
        return carry

    lax.fori_loop(0, ITERS - 1, step, 0)
    out = apply(zcat[0:ROWS, 0:128], zcat[0:ROWS, 128:256], factor())
    out_ref[...] = out[:, 0:RANK]


def subspace(tiles, start, scale):
    return pl.pallas_call(
        functools.partial(subspace_kernel, scale),
        out_shape=jax.ShapeDtypeStruct((ROWS, RANK), F32),
        in_specs=vmem(2),
        out_specs=vmem(1)[0],
        scratch_shapes=[
            pltpu.VMEM((ROWS, 768), BF16),
            pltpu.VMEM((ROWS, 768), BF16),
            pltpu.VMEM((768, 256), BF16),
        ],
        compiler_params=pltpu.CompilerParams(vmem_limit_bytes=48 * 2**20),
        name="subspace",
    )(tiles, start)


def place():
    gx, gy, gz = lax.axis_index("gx"), lax.axis_index("gy"), lax.axis_index("gz")
    return gy, gx // 4, (gx % 4) * 2 + gz // 2, gz % 2


def device(x, y, z, core):
    return (y * 4 + z // 2, x, (z % 2) * 2 + core)


def turn(value, by, size):
    return lax.rem(value + by, size)


def greet(ids):
    barrier = pltpu.get_barrier_semaphore()
    for i in ids:
        pl.semaphore_signal(barrier, inc=1, device_id=i, device_id_type=MESH)
    return len(ids)


def remote(src, dst, send, recv, to):
    copy = pltpu.make_async_remote_copy(
        src_ref=src, dst_ref=dst, send_sem=send, recv_sem=recv, device_id=to, device_id_type=MESH
    )
    copy.start()
    return copy


def local(src, dst, sem):
    pltpu.make_async_copy(src, dst, sem).start()


def await_all(ref, sem):
    pltpu.make_async_copy(ref, ref, sem).wait()


SUM_SCRATCH = [
    pltpu.VMEM((256, 8, 128), F32),
    pltpu.VMEM((128, 8, 128), F32),
    pltpu.VMEM((128, 8, 128), F32),
    pltpu.VMEM((3, 32, 8, 128), F32),
    pltpu.VMEM((3, 8, 8, 128), F32),
    pltpu.VMEM((7, 8, 128), F32),
    pltpu.SemaphoreType.DMA((76,)),
    pltpu.SemaphoreType.DMA((76,)),
]


def sum_everywhere(out, tiles, half, first, second, third, fourth, send, recv):
    x, y, z, core = place()
    flip = core == 0
    a = jnp.where(flip, x, y)
    b = jnp.where(flip, y, x)

    def at(pa, pb, pz, pc):
        return device(jnp.where(flip, pa, pb), jnp.where(flip, pb, pa), pz, pc)

    partner = at(a, b, z, 1 - core)
    peers_a = [at(turn(a, d, 4), b, z, core) for d in range(1, 4)]
    peers_b = [at(a, turn(b, d, 4), z, core) for d in range(1, 4)]
    peers_z = [at(a, b, turn(z, d, 8), core) for d in range(1, 8)]
    mine = core * 128
    other = (1 - core) * 128
    copies = []

    def copy(src, dst, sem, to):
        copies.append(remote(src, dst, send.at[sem], recv.at[sem], to))
        return copies[-1]

    def piece(pa, pb):
        return pa * 32 + pb * 8

    order = (1, 2, 3, 0)
    paired, across = {}, {}
    for e in order:
        for d in order:
            p = piece(turn(b, d, 4), turn(a, e, 4))
            paired[d, e] = copy(tiles.at[pl.ds(other + p, 8)], first.at[pl.ds(p, 8)], 4 * d + e, partner)
    for e in order:
        for d in order:
            paired[d, e].wait_recv()
            p = pl.ds(piece(turn(a, d, 4), turn(b, e, 4)), 8)
            half[p] = tiles[pl.ds(mine + piece(turn(a, d, 4), turn(b, e, 4)), 8)] + first[p]
            if d:
                across[d, e] = copy(half.at[p], second.at[d - 1, pl.ds(turn(b, e, 4) * 8, 8)],
                                    12 + 4 * d + e, peers_a[d - 1])
    along = []
    for e in order:
        for d in range(1, 4):
            across[d, e].wait_recv()
        p = pl.ds(piece(a, turn(b, e, 4)), 8)
        q = pl.ds(turn(b, e, 4) * 8, 8)
        half[p] = half[p] + second[0, q] + second[1, q] + second[2, q]
        if e:
            along.append(copy(half.at[p], third.at[e - 1], 27 + e, peers_b[e - 1]))
    for c in along:
        c.wait_recv()
    home = piece(a, b)
    p = pl.ds(home, 8)
    half[p] = half[p] + third[0] + third[1] + third[2]
    for c in [copy(half.at[home + turn(z, d, 8)], fourth.at[d - 1], 30 + d, peers_z[d - 1]) for d in range(1, 8)]:
        c.wait_recv()
    total = half[home + z]
    for d in range(7):
        total = total + fourth[d]
    own = mine + home + z
    out[own] = total
    for c in [copy(out.at[own], out.at[own], 37 + d, peers_z[d - 1]) for d in range(1, 8)]:
        c.wait_recv()

    def block(d, e):
        return out.at[pl.ds(mine + piece(turn(a, 4 - d, 4), turn(b, 4 - e, 4)), 8)]

    along = [copy(block(0, 0), block(0, 0), 44 + e, peers_b[e - 1]) for e in range(1, 4)]
    across, paired = {}, []
    for e in range(4):
        if e:
            along[e - 1].wait_recv()
        for d in range(1, 4):
            across[d, e] = copy(block(0, e), block(0, e), 44 + 4 * d + e, peers_a[d - 1])
        paired.append(copy(block(0, e), block(0, e), 60 + e, partner))
    for e in range(4):
        for d in range(1, 4):
            across[d, e].wait_recv()
            paired.append(copy(block(d, e), block(d, e), 60 + 4 * d + e, partner))
    for c in paired:
        c.wait_recv()
    for c in copies:
        c.wait_send()


def add_gram(hi, lo, tiles, fresh):
    def put(l, skip, value):
        n = value.shape[0] // 8
        at = pl.ds(BASE[l] + skip // 8, n)
        value = value.reshape(n, 8, 128)
        tiles[at] = value if fresh else tiles[at] + value

    def product(r, c, n):
        return nt(hi[r:], hi[c : c + n]) + nt(hi[r:], lo[c : c + n]) + nt(lo[r:], hi[c : c + n])

    last = product(512, 512, 160)
    lane = lax.broadcasted_iota(jnp.int32, (32, 128), 1)

    def corner(l, value):
        tail = last[128:160, 0:128]
        if l == 4:
            tail = jnp.concatenate([last[128:160, 128:160], jnp.zeros((32, 96), F32)], axis=1)
        tail = pltpu.roll(tail, (96 - 32 * (l % 4)) % 128, 1)
        put(l, 0, jnp.where(lane >= 96, tail, value[0:32]))
        put(l, 32, value[32:])

    block = product(0, 0, 256)
    corner(0, block[:, 0:128])
    corner(1, block[128:, 128:256])
    block = product(256, 256, 256)
    corner(2, block[:, 0:128])
    corner(3, block[128:, 128:256])
    corner(4, last[0:128, 0:128])


def extra_owner(gz, e):
    n = 5 * gz + e
    return ((n // 4 + n) % 4) * 4 + n % 4


def extra_tile():
    gx, gz = lax.axis_index("gx"), lax.axis_index("gz")
    has, which = False, 0
    for e in range(5):
        taken = extra_owner(gz, e) == gx
        has = jnp.logical_or(has, taken)
        which = jnp.where(taken, e, which)
    return has, which


def first_kernel(slab, out, xhi, xlo, rows, tiles, half, first, second, third, fourth, send, recv,
                 slab_send, more_send, slab_recv):
    gx, gy, gz = lax.axis_index("gx"), lax.axis_index("gy"), lax.axis_index("gz")
    x, y, z, core = place()
    ids = [(turn(gx, d, 16), gy, gz) for d in range(1, 16)]
    ids += [device(x, y, z, 1 - core)]
    ids += [device(turn(x, d, 4), y, z, core) for d in range(1, 4)]
    ids += [device(x, y, turn(z, d, 8), core) for d in (1, 3, 5, 7)]
    pl.semaphore_wait(pltpu.get_barrier_semaphore(), greet(ids))

    mine = pl.ds(gx * OWN, OWN)
    for e in range(5):
        to = extra_owner(gz, e)
        src = slab.at[:, pl.ds(128 + 8 * e, 8)]

        @pl.when(to != gx)
        def _():
            remote(src, rows.at[1, mine], more_send.at[e], slab_recv.at[1], (to, gy, gz))

        @pl.when(to == gx)
        def _():
            local(src, rows.at[1, mine], slab_recv.at[1])

    copies = []
    for d in range(1, 16):
        to = turn(gx, d, 16)
        copies.append(remote(slab.at[:, pl.ds(to * 8, 8)], rows.at[0, mine], slab_send.at[d],
                             slab_recv.at[0], (to, gy, gz)))
    local(slab.at[:, pl.ds(gx * 8, 8)], rows.at[0, mine], slab_recv.at[0])

    tiles[...] = jnp.zeros_like(tiles)

    def use(p):
        for j in range(8):
            high, low = split(rows[p, :, j, :])
            xhi[p, :, 128 * j : 128 * j + 128] = high
            xlo[p, :, 128 * j : 128 * j + 128] = low
        add_gram(xhi.at[p], xlo.at[p], tiles, False)

    has, _ = extra_tile()

    @pl.when(has)
    def _():
        await_all(rows.at[1], slab_recv.at[1])
        use(1)

    await_all(rows.at[0], slab_recv.at[0])
    use(0)

    for c in copies:
        c.wait_send()
    for e in range(5):
        to = extra_owner(gz, e)

        @pl.when(to != gx)
        def _():
            src = slab.at[:, pl.ds(128 + 8 * e, 8)]
            await_all(src, more_send.at[e])

    sum_everywhere(out, tiles, half, first, second, third, fourth, send, recv)


def first_gram(slab):
    return pl.pallas_call(
        first_kernel,
        out_shape=(
            jax.ShapeDtypeStruct((256, 8, 128), F32),
            jax.ShapeDtypeStruct((2, ROWS, 1024), BF16),
            jax.ShapeDtypeStruct((2, ROWS, 1024), BF16),
        ),
        in_specs=[pl.BlockSpec(memory_space=pltpu.MemorySpace.HBM)],
        out_specs=tuple(vmem(3)),
        scratch_shapes=[
            pltpu.VMEM((2, ROWS, 8, 128), F32),
            *SUM_SCRATCH,
            pltpu.SemaphoreType.DMA((16,)),
            pltpu.SemaphoreType.DMA((5,)),
            pltpu.SemaphoreType.DMA((2,)),
        ],
        compiler_params=pltpu.CompilerParams(
            collective_id=0, has_side_effects=True, vmem_limit_bytes=48 * 2**20),
        name="first_gram",
    )(slab)


def ranks(gy, core):
    low = gy < 2
    if_zero = (jnp.where(low, 2 * gy, gy + 2), jnp.where(low, 2, 1))
    if_one = (jnp.where(low, gy, 2 * gy - 2), jnp.where(low, 1, 2))
    return jnp.where(core == 0, if_zero[0], if_one[0]), jnp.where(core == 0, if_zero[1], if_one[1])


def owner(r, core):
    zero = (jnp.where(r < 4, r // 2, r - 2), jnp.where(r < 4, r % 2, 0))
    one = (jnp.where(r < 2, r, r // 2 + 1), jnp.where(r < 2, 0, r % 2))
    return jnp.where(core == 0, zero[0], one[0]), jnp.where(core == 0, zero[1], one[1])


def basis_rows(basis):
    wide = jnp.concatenate([basis, jnp.zeros((ROWS, 32), F32)], axis=1)
    high, low = split(wide.T[0:RANK])
    return jnp.concatenate([high, low], axis=0)


def contract(stacked, hi, lo):
    both = nn(stacked, hi)
    return both[0:RANK] + both[RANK:] + nn(stacked[0:RANK], lo)


def second_kernel(basis, xhi, xlo, out, qhi, qlo, part, rows, tiles, half, first, second, third, fourth,
                  send, recv, part_send, part_recv):
    gx, gy, gz = lax.axis_index("gx"), lax.axis_index("gy"), lax.axis_index("gz")
    x, y, z, core = place()
    barrier = pltpu.get_barrier_semaphore()

    def hello(i, carry):
        to = (turn(gx, i // 4, 16), turn(gy, i % 4, 4), gz)
        pl.semaphore_signal(barrier, inc=1, device_id=to, device_id_type=MESH)
        return carry

    lax.fori_loop(1, 64, hello, 0)
    ids = [device(x, y, z, 1 - core)] + [device(x, y, turn(z, d, 8), core) for d in (1, 3, 5, 7)]
    count = 63 + greet(ids)
    stacked = basis_rows(basis[...])
    has, which = extra_tile()

    def work(p):
        for j in range(0, 8, 2):
            at = pl.ds(128 * j, 256)
            value = contract(stacked, xhi[p, :, at], xlo[p, :, at])
            part[p, :, j, :] = value[:, 0:128]
            part[p, :, j + 1, :] = value[:, 128:256]

    def deal(p, tile):
        at = pl.ds(gy * 168 + tile * 8, 8)

        def one(i, carry):
            to_x = turn(gx, i // 6, 16)
            to_y, slot = owner(i % 6, core)
            r = to_x * 6 + i % 6
            me = jnp.logical_and(to_x == gx, to_y == gy)

            @pl.when(jnp.logical_not(me))
            def _():
                remote(part.at[p, r], rows.at[slot, at], part_send.at[p], part_recv.at[0], (to_x, to_y, gz))

            @pl.when(me)
            def _():
                local(part.at[p, r], rows.at[slot, at], part_recv.at[0])

            return carry

        lax.fori_loop(0, RANK, one, 0)

    work(0)
    pl.semaphore_wait(barrier, count)
    deal(0, gx)

    @pl.when(has)
    def _():
        work(1)
        deal(1, 16 + which)

    _, held = ranks(gy, core)

    @pl.when(held == 2)
    def _():
        await_all(rows, part_recv.at[0])
        await_all(part.at[0, pl.ds(0, 94)], part_send.at[0])

        @pl.when(has)
        def _():
            await_all(part.at[1, pl.ds(0, 94)], part_send.at[1])

        high, low = split(rows[1])
        qhi[:, 128:256] = high
        qlo[:, 128:256] = low

    @pl.when(held != 2)
    def _():
        await_all(rows.at[0], part_recv.at[0])
        await_all(part.at[0, pl.ds(0, 95)], part_send.at[0])

        @pl.when(has)
        def _():
            await_all(part.at[1, pl.ds(0, 95)], part_send.at[1])

        qhi[:, 128:256] = jnp.zeros((ROWS, 128), BF16)
        qlo[:, 128:256] = jnp.zeros((ROWS, 128), BF16)

    high, low = split(rows[0])
    qhi[:, 0:128] = high
    qlo[:, 0:128] = low
    add_gram(qhi, qlo, tiles, True)
    sum_everywhere(out, tiles, half, first, second, third, fourth, send, recv)


def second_gram(basis, xhi, xlo):
    return pl.pallas_call(
        second_kernel,
        out_shape=(
            jax.ShapeDtypeStruct((256, 8, 128), F32),
            jax.ShapeDtypeStruct((ROWS, 256), BF16),
            jax.ShapeDtypeStruct((ROWS, 256), BF16),
        ),
        in_specs=vmem(3),
        out_specs=tuple(vmem(3)),
        scratch_shapes=[
            pltpu.VMEM((2, RANK, 8, 128), F32),
            pltpu.VMEM((2, ROWS, 128), F32),
            *SUM_SCRATCH,
            pltpu.SemaphoreType.DMA((2,)),
            pltpu.SemaphoreType.DMA((1,)),
        ],
        compiler_params=pltpu.CompilerParams(
            collective_id=1, has_side_effects=True, vmem_limit_bytes=48 * 2**20),
        name="second_gram",
    )(basis, xhi, xlo)


def core_kernel(basis, qhi, qlo, out, terms, send, recv):
    gx, gy, gz = lax.axis_index("gx"), lax.axis_index("gy"), lax.axis_index("gz")
    barrier = pltpu.get_barrier_semaphore()
    count = greet([(gx, turn(gy, d, 4), gz) for d in range(1, 4)])
    value = contract(basis_rows(basis[...]), qhi[...], qlo[...])
    terms[0] = value[:, 0:128]
    terms[1] = value[:, 128:256]
    start, held = ranks(gy, gz % 2)
    pl.semaphore_wait(barrier, count)

    def deal(k):
        dst = out.at[start + k]
        for d in range(1, 4):
            to = turn(gy, d, 4)
            remote(terms.at[k, pl.ds(to * 24, 24)], dst, send.at[k, d], recv.at[0], (gx, to, gz))
        local(terms.at[k, pl.ds(gy * 24, 24)], dst, recv.at[0])

    def finish(k):
        for d in range(1, 4):
            await_all(terms.at[k, pl.ds(0, 24)], send.at[k, d])

    deal(0)

    @pl.when(held == 2)
    def _():
        deal(1)
        finish(1)

    finish(0)
    await_all(out, recv.at[0])


def core_piece(basis, qhi, qlo):
    return pl.pallas_call(
        core_kernel,
        out_shape=jax.ShapeDtypeStruct((6, 24, 128), F32),
        in_specs=vmem(3),
        out_specs=vmem(1)[0],
        scratch_shapes=[
            pltpu.VMEM((2, RANK, 128), F32),
            pltpu.SemaphoreType.DMA((2, 4)),
            pltpu.SemaphoreType.DMA((1,)),
        ],
        compiler_params=pltpu.CompilerParams(
            collective_id=2, has_side_effects=True, vmem_limit_bytes=48 * 2**20),
        name="core_piece",
    )(basis, qhi, qlo)


def body(slab, start_one, start_two):
    tiles, xhi, xlo = first_gram(slab)
    factor_one = subspace(tiles, start_one, 1.0 / (672 * 512))
    tiles, qhi, qlo = second_gram(factor_one, xhi, xlo)
    factor_two = subspace(tiles, start_two, 1.0 / (RANK * 512))
    return factor_one, factor_two, core_piece(factor_two, qhi, qlo)


def solution(mesh):
    placed = (P("gx", "gy", "gz"), P(), P())
    return jax.shard_map(
        body, mesh=mesh, in_specs=placed, out_specs=(P(), P(), P("gx", "gy", "gz")), check_vma=False
    )
```

```python
import functools
import jax
import jax.numpy as jnp
from jax import lax
from jax.experimental import pallas as pl
from jax.experimental.pallas import tpu as pltpu
from jax.sharding import PartitionSpec as P

RANK = 96
ROWS = 672
ITERS = 8
OWN = 42
LANES = 128
MESH = pl.DeviceIdType.MESH
F32 = jnp.float32
BF16 = jnp.bfloat16
COUNT = (84, 68, 52, 36, 16)
BASE = (0, 84, 152, 204, 240)


def split(value):
    high = value.astype(BF16)
    low = (value - high.astype(F32)).astype(BF16)
    return high, low


def dot(a, b, left, right):
    return lax.dot_general(a, b, (((left,), (right,)), ((), ())), preferred_element_type=F32)


def nt(a, b):
    return dot(a, b, 1, 1)


def nn(a, b):
    return dot(a, b, 1, 0)


def vmem(count):
    return [pl.BlockSpec(memory_space=pltpu.VMEM)] * count


def inverse_factor(square):
    rows = [square[8 * t : 8 * t + 8, :] for t in range(12)]
    lane = lax.broadcasted_iota(jnp.int32, (8, 128), 1)
    sub = lax.broadcasted_iota(jnp.int32, (8, 128), 0)
    aside = [(lane == sub + 8 * t).astype(F32) for t in range(12)]
    done = []
    ahead = [jnp.broadcast_to(rows[0][:, l : l + 1], (8, 128)) for l in range(8)]
    for t in range(12):
        first = 8 * t
        tile, extra = rows[t], aside[t]
        wide = ahead
        cell, line, side, inv = {}, [], [], []
        pivots = None
        for l in range(8):
            for m in range(l, 8):
                cell[m, l] = jnp.broadcast_to(wide[m][l : l + 1, :], (8, 128))
            line.append(jnp.broadcast_to(tile[l : l + 1, :], (8, 128)))
            side.append(jnp.broadcast_to(extra[l : l + 1, :], (8, 128)))
            inv.append(1.0 / cell[l, l])
            pivots = cell[l, l] if l == 0 else jnp.where(sub == l, cell[l, l], pivots)
            if l < 7:
                times = jnp.where(sub > l, wide[l] * inv[l], 0.0)
                for m in range(l + 1, 8):
                    wide[m] = wide[m] - times * cell[m, l]
                tile = tile - times * line[l]
                extra = extra - times * side[l]
        out = extra * lax.rsqrt(pivots)
        done.append(out)
        for u in range(t + 1, 12):
            tail, more = rows[u], aside[u]
            raw, cols = [], []
            for l in range(8):
                value = jnp.broadcast_to(tail[:, first + l : first + l + 1], (8, 128))
                for p in range(l):
                    value = value - cols[p] * cell[l, p]
                raw.append(value)
                cols.append(value * inv[l])
            if u == t + 1:
                ahead = []
                for m in range(8):
                    value = jnp.broadcast_to(tail[:, first + 8 + m : first + 9 + m], (8, 128))
                    for l in range(8):
                        value = value - cols[l] * jnp.broadcast_to(raw[l][m : m + 1, :], (8, 128))
                    ahead.append(value)
            for l in range(8):
                tail = tail - cols[l] * line[l]
                more = more - cols[l] * side[l]
            rows[u], aside[u] = tail, more
    return jnp.concatenate(done, axis=0)


def subspace(scale, tiles_ref, start_ref, out_ref, ghi, glo, zcat):
    def put(r, c, value):
        high, low = split(value)
        ghi[r : r + value.shape[0], c : c + value.shape[1]] = high
        glo[r : r + value.shape[0], c : c + value.shape[1]] = low

    row = lax.broadcasted_iota(jnp.int32, (128, 128), 0)
    col = lax.broadcasted_iota(jnp.int32, (128, 128), 1)
    corner = []
    for l in range(5):
        n = COUNT[l] * 8
        block = tiles_ref[BASE[l] : BASE[l] + COUNT[l]].reshape(n, 128) * scale
        diag = block[0:128]
        put(128 * l, 128 * l, jnp.where(row >= col, diag, diag.T))
        corner.append(pltpu.roll(diag[0:32], (32 + 32 * l) % 128, 1))
        if l < 4:
            rest = block[128:]
            put(128 * l + 128, 128 * l, rest)
            tall = jnp.concatenate([rest, jnp.zeros((96, 128), F32)], axis=0)
            put(128 * l, 128 * l + 128, tall.T)
    lane = lax.broadcasted_iota(jnp.int32, (32, 128), 1)
    left = corner[0]
    for l in range(1, 4):
        left = jnp.where(lane >= 32 * l, corner[l], left)
    right = jnp.where(lane < 32, corner[4], 0.0)
    put(640, 512, left)
    put(640, 640, right)
    put(512, 640, jnp.concatenate([left, jnp.zeros((96, 128), F32)], axis=0).T)
    zcat[ROWS:768] = jnp.zeros((96, 256), BF16)

    def keep(value):
        high, low = split(value)
        zcat[0:ROWS, 0:128] = high
        zcat[0:ROWS, 128:256] = low

    def times_gram():
        both = nn(ghi[...], zcat[...])
        return both[:, 0:128] + both[:, 128:256] + nn(glo[...], zcat[:, 0:128])

    def factor():
        z = zcat[0:ROWS]
        quad = dot(z, z, 0, 0)
        square = quad[0:128, 0:128] + quad[0:128, 128:256] + quad[128:256, 0:128] + quad[128:256, 128:256]
        return inverse_factor(square[0:RANK])

    def apply(high, low, inverse):
        mhi, mlo = split(jnp.concatenate([inverse, jnp.zeros((32, 128), F32)], axis=0))
        lhs = jnp.concatenate([high, low], axis=1)
        return nt(lhs, jnp.concatenate([mhi, mhi], axis=1)) + nt(high, mlo)

    keep(jnp.concatenate([start_ref[...], jnp.zeros((ROWS, 32), F32)], axis=1))
    keep(times_gram())

    def step(_, carry):
        high, low = split(times_gram())
        keep(apply(high, low, factor()))
        return carry

    lax.fori_loop(0, ITERS - 1, step, 0)
    out = apply(zcat[0:ROWS, 0:128], zcat[0:ROWS, 128:256], factor())
    out_ref[...] = out[:, 0:RANK]


def place():
    gx, gy, gz = lax.axis_index("gx"), lax.axis_index("gy"), lax.axis_index("gz")
    return gy, gx // 4, (gx % 4) * 2 + gz // 2, gz % 2


def device(x, y, z, core):
    return (y * 4 + z // 2, x, (z % 2) * 2 + core)


def turn(value, by, size):
    return lax.rem(value + by, size)


def greet(ids):
    barrier = pltpu.get_barrier_semaphore()
    for i in ids:
        pl.semaphore_signal(barrier, inc=1, device_id=i, device_id_type=MESH)
    return len(ids)


def remote(src, dst, send, recv, to):
    copy = pltpu.make_async_remote_copy(
        src_ref=src, dst_ref=dst, send_sem=send, recv_sem=recv, device_id=to, device_id_type=MESH
    )
    copy.start()
    return copy


def local(src, dst, sem):
    pltpu.make_async_copy(src, dst, sem).start()


def await_all(ref, sem):
    pltpu.make_async_copy(ref, ref, sem).wait()


SUM_SCRATCH = [
    pltpu.VMEM((256, 8, 128), F32),
    pltpu.VMEM((128, 8, 128), F32),
    pltpu.VMEM((128, 8, 128), F32),
    pltpu.VMEM((3, 32, 8, 128), F32),
    pltpu.VMEM((3, 8, 8, 128), F32),
    pltpu.VMEM((7, 8, 128), F32),
    pltpu.SemaphoreType.DMA((76,)),
    pltpu.SemaphoreType.DMA((76,)),
]


def sum_everywhere(out, tiles, half, first, second, third, fourth, send, recv):
    x, y, z, core = place()
    flip = core == 0
    a = jnp.where(flip, x, y)
    b = jnp.where(flip, y, x)

    def at(pa, pb, pz, pc):
        return device(jnp.where(flip, pa, pb), jnp.where(flip, pb, pa), pz, pc)

    partner = at(a, b, z, 1 - core)
    peers_a = [at(turn(a, d, 4), b, z, core) for d in range(1, 4)]
    peers_b = [at(a, turn(b, d, 4), z, core) for d in range(1, 4)]
    peers_z = [at(a, b, turn(z, d, 8), core) for d in range(1, 8)]
    mine = core * 128
    other = (1 - core) * 128
    copies = []

    def copy(src, dst, sem, to):
        copies.append(remote(src, dst, send.at[sem], recv.at[sem], to))
        return copies[-1]

    def piece(pa, pb):
        return pa * 32 + pb * 8

    order = (1, 2, 3, 0)
    paired, across = {}, {}
    for e in order:
        for d in order:
            p = piece(turn(b, d, 4), turn(a, e, 4))
            paired[d, e] = copy(tiles.at[pl.ds(other + p, 8)], first.at[pl.ds(p, 8)], 4 * d + e, partner)
    for e in order:
        for d in order:
            paired[d, e].wait_recv()
            p = pl.ds(piece(turn(a, d, 4), turn(b, e, 4)), 8)
            half[p] = tiles[pl.ds(mine + piece(turn(a, d, 4), turn(b, e, 4)), 8)] + first[p]
            if d:
                across[d, e] = copy(half.at[p], second.at[d - 1, pl.ds(turn(b, e, 4) * 8, 8)],
                                    12 + 4 * d + e, peers_a[d - 1])
    along = []
    for e in order:
        for d in range(1, 4):
            across[d, e].wait_recv()
        p = pl.ds(piece(a, turn(b, e, 4)), 8)
        q = pl.ds(turn(b, e, 4) * 8, 8)
        half[p] = half[p] + second[0, q] + second[1, q] + second[2, q]
        if e:
            along.append(copy(half.at[p], third.at[e - 1], 27 + e, peers_b[e - 1]))
    for c in along:
        c.wait_recv()
    home = piece(a, b)
    p = pl.ds(home, 8)
    half[p] = half[p] + third[0] + third[1] + third[2]
    for c in [copy(half.at[home + turn(z, d, 8)], fourth.at[d - 1], 30 + d, peers_z[d - 1]) for d in range(1, 8)]:
        c.wait_recv()
    total = half[home + z]
    for d in range(7):
        total = total + fourth[d]
    own = mine + home + z
    out[own] = total
    for c in [copy(out.at[own], out.at[own], 37 + d, peers_z[d - 1]) for d in range(1, 8)]:
        c.wait_recv()

    def block(d, e):
        return out.at[pl.ds(mine + piece(turn(a, 4 - d, 4), turn(b, 4 - e, 4)), 8)]

    along = [copy(block(0, 0), block(0, 0), 44 + e, peers_b[e - 1]) for e in range(1, 4)]
    across, paired = {}, []
    for e in range(4):
        if e:
            along[e - 1].wait_recv()
        for d in range(1, 4):
            across[d, e] = copy(block(0, e), block(0, e), 44 + 4 * d + e, peers_a[d - 1])
        paired.append(copy(block(0, e), block(0, e), 60 + e, partner))
    for e in range(4):
        for d in range(1, 4):
            across[d, e].wait_recv()
            paired.append(copy(block(d, e), block(d, e), 60 + 4 * d + e, partner))
    for c in paired:
        c.wait_recv()
    for c in copies:
        c.wait_send()


def add_gram(hi, lo, tiles, fresh):
    def put(l, skip, value):
        n = value.shape[0] // 8
        at = pl.ds(BASE[l] + skip // 8, n)
        value = value.reshape(n, 8, 128)
        tiles[at] = value if fresh else tiles[at] + value

    def product(r, c, n):
        return nt(hi[r:], hi[c : c + n]) + nt(hi[r:], lo[c : c + n]) + nt(lo[r:], hi[c : c + n])

    last = product(512, 512, 160)
    lane = lax.broadcasted_iota(jnp.int32, (32, 128), 1)

    def corner(l, value):
        tail = last[128:160, 0:128]
        if l == 4:
            tail = jnp.concatenate([last[128:160, 128:160], jnp.zeros((32, 96), F32)], axis=1)
        tail = pltpu.roll(tail, (96 - 32 * (l % 4)) % 128, 1)
        put(l, 0, jnp.where(lane >= 96, tail, value[0:32]))
        put(l, 32, value[32:])

    block = product(0, 0, 256)
    corner(0, block[:, 0:128])
    corner(1, block[128:, 128:256])
    block = product(256, 256, 256)
    corner(2, block[:, 0:128])
    corner(3, block[128:, 128:256])
    corner(4, last[0:128, 0:128])


def extra_owner(gz, e):
    n = 5 * gz + e
    return ((n // 4 + n) % 4) * 4 + n % 4


def extra_tile():
    gx, gz = lax.axis_index("gx"), lax.axis_index("gz")
    has, which = False, 0
    for e in range(5):
        taken = extra_owner(gz, e) == gx
        has = jnp.logical_or(has, taken)
        which = jnp.where(taken, e, which)
    return has, which


def first_gram(slab, xhi, xlo, rows, tiles, slab_send, more_send, slab_recv):
    gx, gy, gz = lax.axis_index("gx"), lax.axis_index("gy"), lax.axis_index("gz")
    mine = pl.ds(gx * OWN, OWN)
    for e in range(5):
        to = extra_owner(gz, e)
        src = slab.at[:, pl.ds(128 + 8 * e, 8)]

        @pl.when(to != gx)
        def _():
            remote(src, rows.at[1, mine], more_send.at[e], slab_recv.at[1], (to, gy, gz))

        @pl.when(to == gx)
        def _():
            local(src, rows.at[1, mine], slab_recv.at[1])

    copies = []
    for d in range(1, 16):
        to = turn(gx, d, 16)
        copies.append(remote(slab.at[:, pl.ds(to * 8, 8)], rows.at[0, mine], slab_send.at[d],
                             slab_recv.at[0], (to, gy, gz)))
    local(slab.at[:, pl.ds(gx * 8, 8)], rows.at[0, mine], slab_recv.at[0])

    tiles[...] = jnp.zeros_like(tiles)

    def use(p):
        for j in range(8):
            high, low = split(rows[p, :, j, :])
            xhi[p, :, 128 * j : 128 * j + 128] = high
            xlo[p, :, 128 * j : 128 * j + 128] = low
        add_gram(xhi.at[p], xlo.at[p], tiles, False)

    has, _ = extra_tile()

    @pl.when(has)
    def _():
        await_all(rows.at[1], slab_recv.at[1])
        use(1)

    await_all(rows.at[0], slab_recv.at[0])
    use(0)

    for c in copies:
        c.wait_send()
    for e in range(5):
        to = extra_owner(gz, e)

        @pl.when(to != gx)
        def _():
            src = slab.at[:, pl.ds(128 + 8 * e, 8)]
            await_all(src, more_send.at[e])


def ranks(gy, core):
    low = gy < 2
    if_zero = (jnp.where(low, 2 * gy, gy + 2), jnp.where(low, 2, 1))
    if_one = (jnp.where(low, gy, 2 * gy - 2), jnp.where(low, 1, 2))
    return jnp.where(core == 0, if_zero[0], if_one[0]), jnp.where(core == 0, if_zero[1], if_one[1])


def owner(r, core):
    zero = (jnp.where(r < 4, r // 2, r - 2), jnp.where(r < 4, r % 2, 0))
    one = (jnp.where(r < 2, r, r // 2 + 1), jnp.where(r < 2, 0, r % 2))
    return jnp.where(core == 0, zero[0], one[0]), jnp.where(core == 0, zero[1], one[1])


def basis_rows(basis):
    wide = jnp.concatenate([basis, jnp.zeros((ROWS, 32), F32)], axis=1)
    high, low = split(wide.T[0:RANK])
    return jnp.concatenate([high, low], axis=0)


def contract(stacked, hi, lo):
    both = nn(stacked, hi)
    return both[0:RANK] + both[RANK:] + nn(stacked[0:RANK], lo)


def second_gram(basis, xhi, xlo, qhi, qlo, part, rows, tiles, part_send, part_recv):
    gx, gy, gz = lax.axis_index("gx"), lax.axis_index("gy"), lax.axis_index("gz")
    core = gz % 2
    stacked = basis_rows(basis[...])
    has, which = extra_tile()

    def work(p):
        for j in range(0, 8, 2):
            at = pl.ds(128 * j, 256)
            value = contract(stacked, xhi[p, :, at], xlo[p, :, at])
            part[p, :, j, :] = value[:, 0:128]
            part[p, :, j + 1, :] = value[:, 128:256]

    def deal(p, tile):
        at = pl.ds(gy * 168 + tile * 8, 8)

        def one(i, carry):
            to_x = turn(gx, i // 6, 16)
            to_y, slot = owner(i % 6, core)
            r = to_x * 6 + i % 6
            me = jnp.logical_and(to_x == gx, to_y == gy)

            @pl.when(jnp.logical_not(me))
            def _():
                remote(part.at[p, r], rows.at[slot, at], part_send.at[p], part_recv.at[0], (to_x, to_y, gz))

            @pl.when(me)
            def _():
                local(part.at[p, r], rows.at[slot, at], part_recv.at[0])

            return carry

        lax.fori_loop(0, RANK, one, 0)

    work(0)
    deal(0, gx)

    @pl.when(has)
    def _():
        work(1)
        deal(1, 16 + which)

    _, held = ranks(gy, core)

    @pl.when(held == 2)
    def _():
        await_all(rows, part_recv.at[0])
        await_all(part.at[0, pl.ds(0, 94)], part_send.at[0])

        @pl.when(has)
        def _():
            await_all(part.at[1, pl.ds(0, 94)], part_send.at[1])

        high, low = split(rows[1])
        qhi[:, 128:256] = high
        qlo[:, 128:256] = low

    @pl.when(held != 2)
    def _():
        await_all(rows.at[0], part_recv.at[0])
        await_all(part.at[0, pl.ds(0, 95)], part_send.at[0])

        @pl.when(has)
        def _():
            await_all(part.at[1, pl.ds(0, 95)], part_send.at[1])

        qhi[:, 128:256] = jnp.zeros((ROWS, 128), BF16)
        qlo[:, 128:256] = jnp.zeros((ROWS, 128), BF16)

    high, low = split(rows[0])
    qhi[:, 0:128] = high
    qlo[:, 0:128] = low
    add_gram(qhi, qlo, tiles, True)


def core_piece(basis, qhi, qlo, out, terms, send, recv):
    gx, gy, gz = lax.axis_index("gx"), lax.axis_index("gy"), lax.axis_index("gz")
    value = contract(basis_rows(basis[...]), qhi[...], qlo[...])
    terms[0] = value[:, 0:128]
    terms[1] = value[:, 128:256]
    start, held = ranks(gy, gz % 2)

    def deal(k):
        dst = out.at[start + k]
        for d in range(1, 4):
            to = turn(gy, d, 4)
            remote(terms.at[k, pl.ds(to * 24, 24)], dst, send.at[k, d], recv.at[0], (gx, to, gz))
        local(terms.at[k, pl.ds(gy * 24, 24)], dst, recv.at[0])

    def finish(k):
        for d in range(1, 4):
            await_all(terms.at[k, pl.ds(0, 24)], send.at[k, d])

    deal(0)

    @pl.when(held == 2)
    def _():
        deal(1)
        finish(1)

    finish(0)
    await_all(out, recv.at[0])


def arrive():
    gx, gy, gz = lax.axis_index("gx"), lax.axis_index("gy"), lax.axis_index("gz")
    x, y, z, core = place()
    barrier = pltpu.get_barrier_semaphore()

    def hello(i, carry):
        to = (turn(gx, i // 4, 16), turn(gy, i % 4, 4), gz)
        pl.semaphore_signal(barrier, inc=1, device_id=to, device_id_type=MESH)
        return carry

    lax.fori_loop(1, 64, hello, 0)
    ids = [device(x, y, z, 1 - core)] + [device(x, y, turn(z, d, 8), core) for d in (1, 3, 5, 7)]
    pl.semaphore_wait(barrier, 63 + greet(ids))


def kernel(slab, start_one, start_two, factor_one, factor_two, core, xhi, xlo, columns, sums, part, rows, qhi, qlo,
           ghi, glo, zcat, terms, slab_send, more_send, slab_recv, part_send, part_recv, core_send, core_recv, *sum_refs):
    one, two = sum_refs[: len(SUM_SCRATCH)], sum_refs[len(SUM_SCRATCH) :]
    arrive()
    first_gram(slab, xhi, xlo, columns, one[0], slab_send, more_send, slab_recv)
    sum_everywhere(sums.at[0], *one)
    subspace(1.0 / (ROWS * 512), sums.at[0], start_one, factor_one, ghi, glo, zcat)
    second_gram(factor_one, xhi, xlo, qhi, qlo, part, rows, two[0], part_send, part_recv)
    sum_everywhere(sums.at[1], *two)
    subspace(1.0 / (RANK * 512), sums.at[1], start_two, factor_two, ghi, glo, zcat)
    core_piece(factor_two, qhi, qlo, core, terms, core_send, core_recv)


def body(slab, start_one, start_two):
    dma = pltpu.SemaphoreType.DMA
    return pl.pallas_call(
        kernel,
        out_shape=(
            jax.ShapeDtypeStruct((ROWS, RANK), F32),
            jax.ShapeDtypeStruct((ROWS, RANK), F32),
            jax.ShapeDtypeStruct((6, 24, 128), F32),
        ),
        in_specs=[pl.BlockSpec(memory_space=pltpu.MemorySpace.HBM), *vmem(2)],
        out_specs=tuple(vmem(3)),
        scratch_shapes=[
            pltpu.VMEM((2, ROWS, 1024), BF16),
            pltpu.VMEM((2, ROWS, 1024), BF16),
            pltpu.VMEM((2, ROWS, 8, 128), F32),
            pltpu.VMEM((2, 256, 8, 128), F32),
            pltpu.VMEM((2, RANK, 8, 128), F32),
            pltpu.VMEM((2, ROWS, 128), F32),
            pltpu.VMEM((ROWS, 256), BF16),
            pltpu.VMEM((ROWS, 256), BF16),
            pltpu.VMEM((ROWS, 768), BF16),
            pltpu.VMEM((ROWS, 768), BF16),
            pltpu.VMEM((768, 256), BF16),
            pltpu.VMEM((2, RANK, 128), F32),
            dma((16,)),
            dma((5,)),
            dma((2,)),
            dma((2,)),
            dma((1,)),
            dma((2, 4)),
            dma((1,)),
            *SUM_SCRATCH,
            *SUM_SCRATCH,
        ],
        compiler_params=pltpu.CompilerParams(
            collective_id=0, has_side_effects=True, vmem_limit_bytes=48 * 2**20),
        name="hosvd",
    )(slab, start_one, start_two)


def solution(mesh):
    placed = (P("gx", "gy", "gz"), P(), P())
    return jax.shard_map(
        body, mesh=mesh, in_specs=placed, out_specs=(P(), P(), P("gx", "gy", "gz")), check_vma=False
    )
```

```python
import functools
import jax
import jax.numpy as jnp
from jax import lax
from jax.experimental import pallas as pl
from jax.experimental.pallas import tpu as pltpu
from jax.sharding import PartitionSpec as P

RANK = 96
ROWS = 672
ITERS = 8
OWN = 42
LANES = 128
MESH = pl.DeviceIdType.MESH
F32 = jnp.float32
BF16 = jnp.bfloat16
COUNT = (84, 68, 52, 36, 16)
BASE = (0, 84, 152, 204, 240)


def split(value):
    high = value.astype(BF16)
    low = (value - high.astype(F32)).astype(BF16)
    return high, low


def dot(a, b, left, right):
    return lax.dot_general(a, b, (((left,), (right,)), ((), ())), preferred_element_type=F32)


def nt(a, b):
    return dot(a, b, 1, 1)


def nn(a, b):
    return dot(a, b, 1, 0)


def vmem(count):
    return [pl.BlockSpec(memory_space=pltpu.VMEM)] * count


def inverse_factor(square):
    rows = [square[8 * t : 8 * t + 8, :] for t in range(12)]
    lane = lax.broadcasted_iota(jnp.int32, (8, 128), 1)
    sub = lax.broadcasted_iota(jnp.int32, (8, 128), 0)
    aside = [(lane == sub + 8 * t).astype(F32) for t in range(12)]
    done = []
    ahead = [jnp.broadcast_to(rows[0][:, l : l + 1], (8, 128)) for l in range(8)]
    for t in range(12):
        first = 8 * t
        tile, extra = rows[t], aside[t]
        wide = ahead
        cell, line, side, inv = {}, [], [], []
        pivots = None
        for l in range(8):
            for m in range(l, 8):
                cell[m, l] = jnp.broadcast_to(wide[m][l : l + 1, :], (8, 128))
            line.append(jnp.broadcast_to(tile[l : l + 1, :], (8, 128)))
            side.append(jnp.broadcast_to(extra[l : l + 1, :], (8, 128)))
            inv.append(1.0 / cell[l, l])
            pivots = cell[l, l] if l == 0 else jnp.where(sub == l, cell[l, l], pivots)
            if l < 7:
                times = jnp.where(sub > l, wide[l] * inv[l], 0.0)
                for m in range(l + 1, 8):
                    wide[m] = wide[m] - times * cell[m, l]
                tile = tile - times * line[l]
                extra = extra - times * side[l]
        out = extra * lax.rsqrt(pivots)
        done.append(out)
        if t + 3 < 12:
            high, low = split(tile * lax.rsqrt(pivots))
            high_side, low_side = split(extra * lax.rsqrt(pivots))
            left = jnp.concatenate([high, high, low, jnp.zeros_like(low)], axis=0)
            right = jnp.concatenate([high, low, high, jnp.zeros_like(low)], axis=0)
            more = jnp.concatenate([high_side, low_side, high_side, jnp.zeros_like(low)], axis=0)
            change = dot(left, jnp.concatenate([right, more], axis=1), 0, 0)
            for u in range(t + 3, 12):
                rows[u] = rows[u] - change[8 * u : 8 * u + 8, 0:128]
                aside[u] = aside[u] - change[8 * u : 8 * u + 8, 128:256]
        for u in range(t + 1, min(12, t + 3)):
            tail, more = rows[u], aside[u]
            raw, cols = [], []
            for l in range(8):
                if u == t + 1 and t > 0:
                    value = beyond[l]
                else:
                    value = jnp.broadcast_to(tail[:, first + l : first + l + 1], (8, 128))
                for p in range(l):
                    value = value - cols[p] * cell[l, p]
                raw.append(value)
                cols.append(value * inv[l])
            if u == t + 1:
                ahead, spread = [], {}
                for m in range(8):
                    value = jnp.broadcast_to(tail[:, first + 8 + m : first + 9 + m], (8, 128))
                    for l in range(8):
                        spread[l, m] = jnp.broadcast_to(raw[l][m : m + 1, :], (8, 128))
                        value = value - cols[l] * spread[l, m]
                    ahead.append(value)
            if u == t + 2:
                following = []
                for m in range(8):
                    value = jnp.broadcast_to(tail[:, first + 8 + m : first + 9 + m], (8, 128))
                    for l in range(8):
                        value = value - cols[l] * spread[l, m]
                    following.append(value)
            for l in range(8):
                tail = tail - cols[l] * line[l]
                more = more - cols[l] * side[l]
            rows[u], aside[u] = tail, more
        if t + 2 < 12:
            beyond = following
    return jnp.concatenate(done, axis=0)


def subspace(scale, tiles_ref, start_ref, out_ref, ghi, glo, zcat):
    def put(r, c, value):
        high, low = split(value)
        ghi[r : r + value.shape[0], c : c + value.shape[1]] = high
        glo[r : r + value.shape[0], c : c + value.shape[1]] = low

    row = lax.broadcasted_iota(jnp.int32, (128, 128), 0)
    col = lax.broadcasted_iota(jnp.int32, (128, 128), 1)
    corner = []
    for l in range(5):
        n = COUNT[l] * 8
        block = tiles_ref[BASE[l] : BASE[l] + COUNT[l]].reshape(n, 128) * scale
        diag = block[0:128]
        put(128 * l, 128 * l, jnp.where(row >= col, diag, diag.T))
        corner.append(pltpu.roll(diag[0:32], (32 + 32 * l) % 128, 1))
        if l < 4:
            rest = block[128:]
            put(128 * l + 128, 128 * l, rest)
            tall = jnp.concatenate([rest, jnp.zeros((96, 128), F32)], axis=0)
            put(128 * l, 128 * l + 128, tall.T)
    lane = lax.broadcasted_iota(jnp.int32, (32, 128), 1)
    left = corner[0]
    for l in range(1, 4):
        left = jnp.where(lane >= 32 * l, corner[l], left)
    right = jnp.where(lane < 32, corner[4], 0.0)
    put(640, 512, left)
    put(640, 640, right)
    put(512, 640, jnp.concatenate([left, jnp.zeros((96, 128), F32)], axis=0).T)
    zcat[ROWS:768] = jnp.zeros((96, 256), BF16)

    def keep(value):
        high, low = split(value)
        zcat[0:ROWS, 0:128] = high
        zcat[0:ROWS, 128:256] = low

    def times_gram():
        both = nn(ghi[...], zcat[...])
        return both[:, 0:128] + both[:, 128:256] + nn(glo[...], zcat[:, 0:128])

    def factor():
        z = zcat[0:ROWS]
        quad = dot(z, z, 0, 0)
        square = quad[0:128, 0:128] + quad[0:128, 128:256] + quad[128:256, 0:128] + quad[128:256, 128:256]
        return inverse_factor(square[0:RANK])

    def apply(high, low, inverse):
        mhi, mlo = split(jnp.concatenate([inverse, jnp.zeros((32, 128), F32)], axis=0))
        lhs = jnp.concatenate([high, low], axis=1)
        return nt(lhs, jnp.concatenate([mhi, mhi], axis=1)) + nt(high, mlo)

    keep(start_ref[...])
    keep(times_gram())

    def step(_, carry):
        high, low = split(times_gram())
        keep(apply(high, low, factor()))
        return carry

    lax.fori_loop(0, ITERS - 1, step, 0)
    high, low = split(factor())
    z = zcat[0:ROWS]
    out_ref[...] = nt(jnp.concatenate([high, high], axis=1), z) + nt(low, z[:, 0:128])


def place():
    gx, gy, gz = lax.axis_index("gx"), lax.axis_index("gy"), lax.axis_index("gz")
    return gy, gx // 4, (gx % 4) * 2 + gz // 2, gz % 2


def device(x, y, z, core):
    return (y * 4 + z // 2, x, (z % 2) * 2 + core)


def turn(value, by, size):
    return lax.rem(value + by, size)


def greet(ids):
    barrier = pltpu.get_barrier_semaphore()
    for i in ids:
        pl.semaphore_signal(barrier, inc=1, device_id=i, device_id_type=MESH)
    return len(ids)


def remote(src, dst, send, recv, to):
    copy = pltpu.make_async_remote_copy(
        src_ref=src, dst_ref=dst, send_sem=send, recv_sem=recv, device_id=to, device_id_type=MESH
    )
    copy.start()
    return copy


def local(src, dst, sem):
    pltpu.make_async_copy(src, dst, sem).start()


def await_all(ref, sem):
    pltpu.make_async_copy(ref, ref, sem).wait()


SUM_SCRATCH = [
    pltpu.VMEM((256, 8, 128), F32),
    pltpu.VMEM((128, 8, 128), F32),
    pltpu.VMEM((128, 8, 128), F32),
    pltpu.VMEM((3, 32, 8, 128), F32),
    pltpu.VMEM((3, 8, 8, 128), F32),
    pltpu.VMEM((7, 8, 128), F32),
    pltpu.SemaphoreType.DMA((76,)),
    pltpu.SemaphoreType.DMA((76,)),
]


def sum_everywhere(out, tiles, half, first, second, third, fourth, send, recv):
    x, y, z, core = place()
    flip = core == 0
    a = jnp.where(flip, x, y)
    b = jnp.where(flip, y, x)

    def at(pa, pb, pz, pc):
        return device(jnp.where(flip, pa, pb), jnp.where(flip, pb, pa), pz, pc)

    partner = at(a, b, z, 1 - core)
    peers_a = [at(turn(a, d, 4), b, z, core) for d in range(1, 4)]
    peers_b = [at(a, turn(b, d, 4), z, core) for d in range(1, 4)]
    peers_z = [at(a, b, turn(z, d, 8), core) for d in range(1, 8)]
    mine = core * 128
    other = (1 - core) * 128
    copies = []

    def copy(src, dst, sem, to):
        copies.append(remote(src, dst, send.at[sem], recv.at[sem], to))
        return copies[-1]

    def piece(pa, pb):
        return pa * 32 + pb * 8

    order = (1, 2, 3, 0)
    paired, across = {}, {}
    for e in order:
        for d in order:
            p = piece(turn(b, d, 4), turn(a, e, 4))
            paired[d, e] = copy(tiles.at[pl.ds(other + p, 8)], first.at[pl.ds(p, 8)], 4 * d + e, partner)
    for e in order:
        for d in order:
            paired[d, e].wait_recv()
            p = pl.ds(piece(turn(a, d, 4), turn(b, e, 4)), 8)
            half[p] = tiles[pl.ds(mine + piece(turn(a, d, 4), turn(b, e, 4)), 8)] + first[p]
            if d:
                across[d, e] = copy(half.at[p], second.at[d - 1, pl.ds(turn(b, e, 4) * 8, 8)],
                                    12 + 4 * d + e, peers_a[d - 1])
    along = []
    for e in order:
        for d in range(1, 4):
            across[d, e].wait_recv()
        p = pl.ds(piece(a, turn(b, e, 4)), 8)
        q = pl.ds(turn(b, e, 4) * 8, 8)
        half[p] = half[p] + second[0, q] + second[1, q] + second[2, q]
        if e:
            along.append(copy(half.at[p], third.at[e - 1], 27 + e, peers_b[e - 1]))
    for c in along:
        c.wait_recv()
    home = piece(a, b)
    p = pl.ds(home, 8)
    half[p] = half[p] + third[0] + third[1] + third[2]
    for c in [copy(half.at[home + turn(z, d, 8)], fourth.at[d - 1], 30 + d, peers_z[d - 1]) for d in range(1, 8)]:
        c.wait_recv()
    total = half[home + z]
    for d in range(7):
        total = total + fourth[d]
    own = mine + home + z
    out[own] = total
    for c in [copy(out.at[own], out.at[own], 37 + d, peers_z[d - 1]) for d in range(1, 8)]:
        c.wait_recv()

    def block(d, e):
        return out.at[pl.ds(mine + piece(turn(a, 4 - d, 4), turn(b, 4 - e, 4)), 8)]

    along = [copy(block(0, 0), block(0, 0), 44 + e, peers_b[e - 1]) for e in range(1, 4)]
    across, paired = {}, []
    for e in range(4):
        if e:
            along[e - 1].wait_recv()
        for d in range(1, 4):
            across[d, e] = copy(block(0, e), block(0, e), 44 + 4 * d + e, peers_a[d - 1])
        paired.append(copy(block(0, e), block(0, e), 60 + e, partner))
    for e in range(4):
        for d in range(1, 4):
            across[d, e].wait_recv()
            paired.append(copy(block(d, e), block(d, e), 60 + 4 * d + e, partner))
    for c in paired:
        c.wait_recv()
    for c in copies:
        c.wait_send()


def add_gram(hi, lo, tiles, fresh):
    def put(l, skip, value):
        n = value.shape[0] // 8
        at = pl.ds(BASE[l] + skip // 8, n)
        value = value.reshape(n, 8, 128)
        tiles[at] = value if fresh else tiles[at] + value

    def product(r, c, n):
        return nt(hi[r:], hi[c : c + n]) + nt(hi[r:], lo[c : c + n]) + nt(lo[r:], hi[c : c + n])

    last = product(512, 512, 160)
    lane = lax.broadcasted_iota(jnp.int32, (32, 128), 1)

    def corner(l, value):
        tail = last[128:160, 0:128]
        if l == 4:
            tail = jnp.concatenate([last[128:160, 128:160], jnp.zeros((32, 96), F32)], axis=1)
        tail = pltpu.roll(tail, (96 - 32 * (l % 4)) % 128, 1)
        put(l, 0, jnp.where(lane >= 96, tail, value[0:32]))
        put(l, 32, value[32:])

    block = product(0, 0, 256)
    corner(0, block[:, 0:128])
    corner(1, block[128:, 128:256])
    block = product(256, 256, 256)
    corner(2, block[:, 0:128])
    corner(3, block[128:, 128:256])
    corner(4, last[0:128, 0:128])


def extra_owner(gz, e):
    n = 5 * gz + e
    return ((n // 4 + n) % 4) * 4 + n % 4


def extra_tile():
    gx, gz = lax.axis_index("gx"), lax.axis_index("gz")
    has, which = False, 0
    for e in range(5):
        taken = extra_owner(gz, e) == gx
        has = jnp.logical_or(has, taken)
        which = jnp.where(taken, e, which)
    return has, which


def first_gram(slab, xhi, xlo, rows, tiles, slab_send, more_send, slab_recv, meanwhile):
    gx, gy, gz = lax.axis_index("gx"), lax.axis_index("gy"), lax.axis_index("gz")
    mine = pl.ds(gx * OWN, OWN)
    for e in range(5):
        to = extra_owner(gz, e)
        src = slab.at[:, pl.ds(128 + 8 * e, 8)]

        @pl.when(to != gx)
        def _():
            remote(src, rows.at[1, mine], more_send.at[e], slab_recv.at[1], (to, gy, gz))

        @pl.when(to == gx)
        def _():
            local(src, rows.at[1, mine], slab_recv.at[1])

    copies = []
    for d in range(1, 16):
        to = turn(gx, d, 16)
        copies.append(remote(slab.at[:, pl.ds(to * 8, 8)], rows.at[0, mine], slab_send.at[d],
                             slab_recv.at[0], (to, gy, gz)))
    local(slab.at[:, pl.ds(gx * 8, 8)], rows.at[0, mine], slab_recv.at[0])

    tiles[...] = jnp.zeros_like(tiles)
    meanwhile()

    def use(p):
        for j in range(8):
            high, low = split(rows[p, :, j, :])
            xhi[p, :, 128 * j : 128 * j + 128] = high
            xlo[p, :, 128 * j : 128 * j + 128] = low
        add_gram(xhi.at[p], xlo.at[p], tiles, False)

    has, _ = extra_tile()

    @pl.when(has)
    def _():
        await_all(rows.at[1], slab_recv.at[1])
        use(1)

    await_all(rows.at[0], slab_recv.at[0])
    use(0)

    def finish():
        for c in copies:
            c.wait_send()
        for e in range(5):

            @pl.when(extra_owner(gz, e) != gx)
            def _():
                await_all(slab.at[:, pl.ds(128 + 8 * e, 8)], more_send.at[e])

    return finish


def ranks(gy, core):
    low = gy < 2
    if_zero = (jnp.where(low, 2 * gy, gy + 2), jnp.where(low, 2, 1))
    if_one = (jnp.where(low, gy, 2 * gy - 2), jnp.where(low, 1, 2))
    return jnp.where(core == 0, if_zero[0], if_one[0]), jnp.where(core == 0, if_zero[1], if_one[1])


def owner(r, core):
    zero = (jnp.where(r < 4, r // 2, r - 2), jnp.where(r < 4, r % 2, 0))
    one = (jnp.where(r < 2, r, r // 2 + 1), jnp.where(r < 2, 0, r % 2))
    return jnp.where(core == 0, zero[0], one[0]), jnp.where(core == 0, zero[1], one[1])


def basis_rows(basis):
    return jnp.concatenate(split(basis), axis=0)


def contract(stacked, hi, lo):
    both = nn(stacked, hi)
    return both[0:RANK] + both[RANK:] + nn(stacked[0:RANK], lo)


def second_gram(basis, xhi, xlo, qhi, qlo, part, rows, tiles, part_send, part_recv):
    gx, gy, gz = lax.axis_index("gx"), lax.axis_index("gy"), lax.axis_index("gz")
    core = gz % 2
    stacked = basis_rows(basis[...])
    has, which = extra_tile()

    def work(p):
        for j in range(0, 8, 2):
            at = pl.ds(128 * j, 256)
            value = contract(stacked, xhi[p, :, at], xlo[p, :, at])
            part[p, :, j, :] = value[:, 0:128]
            part[p, :, j + 1, :] = value[:, 128:256]

    def deal(p, tile):
        at = pl.ds(gy * 168 + tile * 8, 8)

        def one(i, carry):
            to_x = turn(gx, i // 6, 16)
            to_y, slot = owner(i % 6, core)
            r = to_x * 6 + i % 6
            me = jnp.logical_and(to_x == gx, to_y == gy)

            @pl.when(jnp.logical_not(me))
            def _():
                remote(part.at[p, r], rows.at[slot, at], part_send.at[p], part_recv.at[0], (to_x, to_y, gz))

            @pl.when(me)
            def _():
                local(part.at[p, r], rows.at[slot, at], part_recv.at[0])

            return carry

        lax.fori_loop(0, RANK, one, 0)

    work(0)
    deal(0, gx)

    @pl.when(has)
    def _():
        work(1)
        deal(1, 16 + which)

    _, held = ranks(gy, core)

    @pl.when(held == 2)
    def _():
        await_all(rows, part_recv.at[0])
        high, low = split(rows[1])
        qhi[:, 128:256] = high
        qlo[:, 128:256] = low

    @pl.when(held != 2)
    def _():
        await_all(rows.at[0], part_recv.at[0])
        qhi[:, 128:256] = jnp.zeros((ROWS, 128), BF16)
        qlo[:, 128:256] = jnp.zeros((ROWS, 128), BF16)

    def finish():
        for count in (1, 2):

            @pl.when(held == count)
            def _():
                sent = pl.ds(0, RANK - count)
                await_all(part.at[0, sent], part_send.at[0])

                @pl.when(has)
                def _():
                    await_all(part.at[1, sent], part_send.at[1])

    high, low = split(rows[0])
    qhi[:, 0:128] = high
    qlo[:, 0:128] = low
    add_gram(qhi, qlo, tiles, True)
    return finish


def core_piece(basis, qhi, qlo, out, terms, send, recv):
    gx, gy, gz = lax.axis_index("gx"), lax.axis_index("gy"), lax.axis_index("gz")
    value = contract(basis_rows(basis[...]), qhi[...], qlo[...])
    terms[0] = value[:, 0:128]
    terms[1] = value[:, 128:256]
    start, held = ranks(gy, gz % 2)

    def deal(k):
        dst = out.at[start + k]
        for d in range(1, 4):
            to = turn(gy, d, 4)
            remote(terms.at[k, pl.ds(to * 24, 24)], dst, send.at[k, d], recv.at[0], (gx, to, gz))
        local(terms.at[k, pl.ds(gy * 24, 24)], dst, recv.at[0])

    def finish(k):
        for d in range(1, 4):
            await_all(terms.at[k, pl.ds(0, 24)], send.at[k, d])

    deal(0)

    @pl.when(held == 2)
    def _():
        deal(1)
        finish(1)

    finish(0)
    await_all(out, recv.at[0])


def arrive():
    gx, gy, gz = lax.axis_index("gx"), lax.axis_index("gy"), lax.axis_index("gz")
    x, y, z, core = place()
    barrier = pltpu.get_barrier_semaphore()

    def hello(i, carry):
        to = (turn(gx, i // 4, 16), turn(gy, i % 4, 4), gz)
        pl.semaphore_signal(barrier, inc=1, device_id=to, device_id_type=MESH)
        return carry

    lax.fori_loop(32, 64, hello, 0)
    lax.fori_loop(1, 32, hello, 0)
    ids = [device(x, y, z, 1 - core)] + [device(x, y, turn(z, d, 8), core) for d in (1, 3, 5, 7)]
    pl.semaphore_wait(barrier, 63 + greet(ids))


def kernel(slab, start_one, start_two, factor_one, factor_two, core, flat, starts, start_sem, xhi, xlo, columns, sums, part, rows, qhi, qlo,
           ghi, glo, zcat, terms, slab_send, more_send, slab_recv, part_send, part_recv, core_send, core_recv, *sum_refs):
    one, two = sum_refs[: len(SUM_SCRATCH)], sum_refs[len(SUM_SCRATCH) :]
    pltpu.make_async_copy(start_one, flat.at[0], start_sem.at[0]).start()
    pltpu.make_async_copy(start_two, flat.at[1], start_sem.at[1]).start()
    arrive()

    def turn_starts():
        for n in range(2):
            await_all(flat.at[n], start_sem.at[n])
            wide = jnp.concatenate([flat[n], jnp.zeros((RANK, 96), F32)], axis=1)
            wide = jnp.concatenate([wide, jnp.zeros((32, 768), F32)], axis=0)
            starts[n] = wide.T[0:ROWS]

    sent_slab = first_gram(slab, xhi, xlo, columns, one[0], slab_send, more_send, slab_recv, turn_starts)
    sum_everywhere(sums.at[0], *one)
    subspace(1.0 / (ROWS * 512), sums.at[0], starts.at[0], factor_one, ghi, glo, zcat)
    sent_parts = second_gram(factor_one, xhi, xlo, qhi, qlo, part, rows, two[0], part_send, part_recv)
    sum_everywhere(sums.at[1], *two)
    subspace(1.0 / (RANK * 512), sums.at[1], starts.at[1], factor_two, ghi, glo, zcat)
    core_piece(factor_two, qhi, qlo, core, terms, core_send, core_recv)
    sent_slab()
    sent_parts()


def body(slab, start_one, start_two):
    dma = pltpu.SemaphoreType.DMA
    one, two, core = pl.pallas_call(
        kernel,
        out_shape=(
            jax.ShapeDtypeStruct((RANK, ROWS), F32),
            jax.ShapeDtypeStruct((RANK, ROWS), F32),
            jax.ShapeDtypeStruct((6, 24, 128), F32),
        ),
        in_specs=[pl.BlockSpec(memory_space=pltpu.MemorySpace.HBM)] * 3,
        out_specs=tuple(vmem(3)),
        scratch_shapes=[
            pltpu.VMEM((2, RANK, ROWS), F32),
            pltpu.VMEM((2, ROWS, 128), F32),
            dma((2,)),
            pltpu.VMEM((2, ROWS, 1024), BF16),
            pltpu.VMEM((2, ROWS, 1024), BF16),
            pltpu.VMEM((2, ROWS, 8, 128), F32),
            pltpu.VMEM((2, 256, 8, 128), F32),
            pltpu.VMEM((2, RANK, 8, 128), F32),
            pltpu.VMEM((2, ROWS, 128), F32),
            pltpu.VMEM((ROWS, 256), BF16),
            pltpu.VMEM((ROWS, 256), BF16),
            pltpu.VMEM((ROWS, 768), BF16),
            pltpu.VMEM((ROWS, 768), BF16),
            pltpu.VMEM((768, 256), BF16),
            pltpu.VMEM((2, RANK, 128), F32),
            dma((16,)),
            dma((5,)),
            dma((2,)),
            dma((2,)),
            dma((1,)),
            dma((2, 4)),
            dma((1,)),
            *SUM_SCRATCH,
            *SUM_SCRATCH,
        ],
        compiler_params=pltpu.CompilerParams(
            collective_id=0, has_side_effects=True, vmem_limit_bytes=48 * 2**20),
        name="hosvd",
    )(slab, start_one.T, start_two.T)
    return one.T, two.T, core


def solution(mesh):
    placed = (P("gx", "gy", "gz"), P(), P())
    return jax.shard_map(
        body, mesh=mesh, in_specs=placed, out_specs=(P(), P(), P("gx", "gy", "gz")), check_vma=False
    )
```
